32 devices in a mesh: dom: 2 (over x), dp: 2 (over core), tp: 8 (over z, y).
Axes of the slice: x: 2, y: 2, z: 4, core: 2. Of those that a mesh axis runs over, the one named last changes fastest.
Arguments:
- layer_input_rows: bfloat16 [3072, 8192], P(('dom', 'dp'), 'tp'), parts along dimension 0, may hold values from -6 to 6
- cotangent: bfloat16 [3072, 29568], P(('dom', 'dp'), 'tp'), parts along dimension 0, may hold values from -6 to 6
- frozen_up_matrix: bfloat16 [8192, 29568], P('dp', 'tp'), may hold values from -0.03125 to 0.03125
- adapter_down_matrices: bfloat16 [24, 16, 8192], P('dom', None, 'tp'), parts along dimension 0, may hold values from -0.1875 to 0.1875
- adapter_up_matrices: bfloat16 [24, 16, 29568], P('dom', None, 'tp'), parts along dimension 0, may hold values from -0.03125 to 0.03125
- row_adapter_index: int32 [3072], P(('dom', 'dp')), parts along dimension 0, may hold values from 0 to 11, as said below
- counts: int32 [4, 12], P(('dom', 'dp')), parts along dimension 0, may hold values from 0 to 256, as said below
- offsets: int32 [4, 12], P(('dom', 'dp')), parts along dimension 0, may hold values from 0 to 6
- gradient_owner_slot: int32 [24], P('dom'), parts along dimension 0, may hold values from 0 to 11, each once
Outputs:
- input_gradient: bfloat16 [3072, 8192], P(('dom', 'dp'), 'tp'), parts along dimension 0
- owned_down: float32 [24, 16, 8192], P(('dom', 'dp'), None, 'tp'), parts along dimension 0
- owned_up: float32 [24, 16, 29568], P(('dom', 'dp'), None, 'tp'), parts along dimension 0
The draws below stay inside these ranges and needn't reach their ends.
There are 2 independent parts, one for each index of `dom`. The reference program is written for one: setup_inputs(seed, part) draws one part's arguments, and reference() takes and returns one part's arrays. A program takes and returns all parts, laid end to end along the dimension named above; an argument that names none is the same for every part. Nothing has to cross between parts.
Inputs may be any that keep to these rules, and one draw needn't show every extreme that they name: In each replica the rows are laid out in blocks of 128, every block belonging to some adapter: the rows of adapter a with counts > 0 fill blocks offsets[r, a] onward, its first counts rows live and the rest of its last block padding; an adapter's blocks are consecutive and never shared; an adapter with no tokens has offsets equal to the number of blocks. Each adapter holds at most two blocks in a replica. `row_adapter_index`: equal for all rows of a block. `gradient_owner_slot`: each slot holds one adapter.
All inputs are finite; a program needn't handle non-finite values.
Results may differ from the reference program's by a relative error of at most 0.015.
Values may be sent and summed in bfloat16 or wider, within the bound.
No kernel may reach another device: no remote copies, remote signals or barrier semaphores. Data moves between devices by JAX's collectives and lax.ppermute only.
A program may use at most 256 MiB of HBM per device.

```python
import jax
import jax.numpy as jnp
from jax import lax

MODEL_WIDTH = 8192
HIDDEN_UNITS = 29568
ADAPTER_RANK = 16
BLOCK = 128
TOKEN_ROWS_LOCAL = 768
TOKENS = 1536
ADAPTER_COUNT = 12
N_DP = 2
N_TP = 8


def layout_plan(key):
    block_total = TOKEN_ROWS_LOCAL // BLOCK

    def replica_plan(replica_key, replica):
        key_extra = jax.random.fold_in(replica_key, 1)
        key_order = jax.random.fold_in(replica_key, 2)
        key_fill = jax.random.fold_in(replica_key, 3)
        used = jnp.int32(block_total)
        extra = jax.random.randint(key_extra, (), 0, block_total // 4 + 1)
        extra = jnp.where(replica == 0, jnp.maximum(extra, min(1, block_total // 2)), extra).astype(jnp.int32)
        kinds = used - extra
        order = jax.random.permutation(key_order, ADAPTER_COUNT).astype(jnp.int32)
        slot = jnp.arange(ADAPTER_COUNT, dtype=jnp.int32)
        present = slot < kinds
        block_span = jnp.where(slot < extra, 2, 1)
        first_block = slot + jnp.minimum(slot, extra)
        fill = jax.random.randint(key_fill, (ADAPTER_COUNT,), 1, BLOCK + 1)
        fill = jnp.where((replica == 0) & (slot == 0), BLOCK, fill)
        live_count = jnp.where(present, (block_span - 1) * BLOCK + fill, 0).astype(jnp.int32)
        start_block = jnp.where(present, first_block, used).astype(jnp.int32)
        counts_row = jnp.zeros((ADAPTER_COUNT,), jnp.int32).at[order].set(live_count)
        offsets_row = jnp.zeros((ADAPTER_COUNT,), jnp.int32).at[order].set(start_block)
        block_index = jnp.arange(block_total, dtype=jnp.int32)
        owner_index = jnp.where(block_index < 2 * extra, block_index // 2, block_index - extra)
        owner_index = jnp.minimum(owner_index, ADAPTER_COUNT - 1)
        block_adapter = order[owner_index].astype(jnp.int32)
        return (jnp.repeat(block_adapter, BLOCK), counts_row, offsets_row)
    subkeys = jax.random.split(key, N_DP)
    return jax.vmap(replica_plan)(subkeys, jnp.arange(N_DP, dtype=jnp.int32))


def draw_row_adapter_index(key, part):
    adapter_rows, counts_all, offsets_all = layout_plan(key)
    return adapter_rows.reshape(TOKENS).astype(jnp.int32)


def draw_counts(key, part):
    adapter_rows, counts_all, offsets_all = layout_plan(key)
    return counts_all.astype(jnp.int32)


def draw_offsets(key, part):
    adapter_rows, counts_all, offsets_all = layout_plan(key)
    return offsets_all.astype(jnp.int32)


def steps_of(rng, shape, cuts, smallest, top_value):
    factor_of = 1.0
    for axis_at, blocks in cuts:
        draws = jax.random.uniform(jax.random.fold_in(jax.random.fold_in(rng, 6), axis_at), (blocks,), jnp.float32, smallest / len(cuts), top_value / len(cuts))
        factor_of = factor_of * jnp.repeat(jnp.exp(draws), shape[axis_at] // blocks).reshape((-1,) + (1,) * (len(shape) - 1 - axis_at))
    return factor_of


def noise(rng, extent, spread, most, cuts=(), kind=jnp.bfloat16):
    result = spread * jax.random.normal(rng, extent, jnp.float32)
    if cuts:
        result = result * steps_of(rng, extent, cuts, -0.22, 0.18)
    return jnp.clip(result, -most, most).astype(kind)


def setup_inputs(seed: int = 0, part: int = 0) -> dict:
    arg_keys = jax.random.split(jax.random.key(seed), 10)
    part_keys = jax.random.split(jax.random.fold_in(arg_keys[9], part), 10)
    layer_input_rows = noise(part_keys[0], (TOKENS, MODEL_WIDTH), 1.0, 6.0, ((0, 2), (1, 8)))
    cotangent = noise(part_keys[1], (TOKENS, HIDDEN_UNITS), 1.0, 6.0, ((0, 2), (1, 8)))
    frozen_up_matrix = noise(arg_keys[2], (MODEL_WIDTH, HIDDEN_UNITS), HIDDEN_UNITS ** -0.5, 0.03125, ((0, 2), (1, 8)))
    adapter_down_matrices = noise(part_keys[3], (ADAPTER_COUNT, ADAPTER_RANK, MODEL_WIDTH), 1024 ** -0.5, 0.1875, ((2, 8),))
    adapter_up_matrices = noise(part_keys[4], (ADAPTER_COUNT, ADAPTER_RANK, HIDDEN_UNITS), HIDDEN_UNITS ** -0.5, 0.03125, ((2, 8),))
    row_adapter_index = draw_row_adapter_index(jax.random.fold_in(jax.random.fold_in(arg_keys[9], part), 71), part)
    counts = draw_counts(jax.random.fold_in(jax.random.fold_in(arg_keys[9], part), 71), part)
    offsets = draw_offsets(jax.random.fold_in(jax.random.fold_in(arg_keys[9], part), 71), part)
    gradient_owner_slot = jax.random.permutation(part_keys[8], ADAPTER_COUNT).astype(jnp.int32)
    return {"layer_input_rows": layer_input_rows, "cotangent": cotangent, "frozen_up_matrix": frozen_up_matrix, "adapter_down_matrices": adapter_down_matrices, "adapter_up_matrices": adapter_up_matrices, "row_adapter_index": row_adapter_index, "counts": counts, "offsets": offsets, "gradient_owner_slot": gradient_owner_slot}


ADAPTER_SCALE = 0.5


def reference(layer_input_rows, cotangent, frozen_up_matrix, adapter_down_matrices, adapter_up_matrices, row_adapter_index, counts, offsets, gradient_owner_slot):
    position = jnp.arange(N_DP * TOKEN_ROWS_LOCAL, dtype=jnp.int32)
    replica = position // TOKEN_ROWS_LOCAL
    within = position % TOKEN_ROWS_LOCAL
    clamped = jnp.minimum(row_adapter_index, ADAPTER_COUNT - 1).astype(jnp.int32)
    first_row = offsets[replica, clamped] * BLOCK
    live_count = counts[replica, clamped]
    active_mask = (row_adapter_index < ADAPTER_COUNT) & (within >= first_row) & (within - first_row < live_count)
    block_adapter = row_adapter_index.reshape(-1, BLOCK)[:, 0]
    block_bounded = jnp.minimum(block_adapter, ADAPTER_COUNT - 1).astype(jnp.int32)
    blocks = block_adapter.shape[0]
    down_block_grads = adapter_down_matrices[block_bounded].astype(jnp.float32)
    up_block_grads = adapter_up_matrices[block_bounded].astype(jnp.float32)
    hidden_blocks = layer_input_rows.reshape(blocks, BLOCK, MODEL_WIDTH).astype(jnp.float32)
    cot_blocks = cotangent.reshape(blocks, BLOCK, HIDDEN_UNITS).astype(jnp.float32)
    mask_blocks = active_mask.reshape(blocks, BLOCK, 1)
    reduced = jnp.where(mask_blocks, jnp.einsum('btd,brd->btr', hidden_blocks, down_block_grads), 0.0).astype(jnp.bfloat16)
    backward_lowrank = jnp.where(mask_blocks, jnp.einsum('btf,brf->btr', cot_blocks, up_block_grads), 0.0).astype(jnp.bfloat16)

    piece_width = HIDDEN_UNITS // N_TP

    def add_piece(shard_index, total):
        begin_at = (shard_index * piece_width).astype(jnp.int32)
        cot_piece = lax.dynamic_slice_in_dim(cotangent, begin_at, piece_width, 1)
        weight_piece = lax.dynamic_slice_in_dim(frozen_up_matrix, begin_at, piece_width, 1)
        product = lax.dot_general(cot_piece, weight_piece, (((1,), (1,)), ((), ())), preferred_element_type=jnp.float32)
        rounded = lax.optimization_barrier(product.astype(jnp.bfloat16))
        return total + rounded.astype(jnp.float32)

    frozen_output = lax.fori_loop(0, N_TP, add_piece, jnp.zeros((N_DP * TOKEN_ROWS_LOCAL, MODEL_WIDTH), jnp.float32))
    adapter_contribution = jnp.einsum('ays,asf->ayf', backward_lowrank.astype(jnp.float32), down_block_grads).reshape(N_DP * TOKEN_ROWS_LOCAL, MODEL_WIDTH)
    input_gradient = jnp.where(active_mask[:, None], frozen_output + ADAPTER_SCALE * adapter_contribution, 0.0).astype(jnp.bfloat16)

    adapter_indicator = jax.nn.one_hot(block_adapter, ADAPTER_COUNT, dtype=jnp.float32)
    blockwise_up_grad = jnp.einsum('btr,btf->brf', reduced.astype(jnp.float32), cot_blocks)
    blockwise_down_grad = jnp.einsum('btr,btd->brd', backward_lowrank.astype(jnp.float32), hidden_blocks)
    up_gradient = ADAPTER_SCALE * jnp.einsum('ou,ody->udy', adapter_indicator, blockwise_up_grad, precision=lax.Precision.HIGHEST)
    down_gradient = ADAPTER_SCALE * jnp.einsum('pi,pom->iom', adapter_indicator, blockwise_down_grad, precision=lax.Precision.HIGHEST)
    owned_down = jnp.zeros_like(down_gradient).at[gradient_owner_slot].set(down_gradient)
    owned_up = jnp.zeros_like(up_gradient).at[gradient_owner_slot].set(up_gradient)
    return input_gradient, owned_down, owned_up
```

```python
import functools

import jax
import jax.numpy as jnp
from jax import lax
from jax.experimental import pallas as pl
from jax.experimental.pallas import tpu as pltpu
from jax.sharding import PartitionSpec as P

BLOCK = 128
ADAPTER_SCALE = 0.5
VMEM_LIMIT = 32 << 20
VMEM_SPARE = 4 << 20
PIECE = 1280
SIZES = ((18, 11), (24, 12))
OWN_CUTS = (2, 6)
SHARED_CUTS = (4, 3, 1)


def dot(a, b, dims):
    return lax.dot_general(a, b, (dims, ((), ())), preferred_element_type=jnp.float32)


def project(weights, starts, tasks, after=None):
    picked = starts.shape[1]
    pieces, _, filled = tasks[0][0].shape
    length = weights.shape[0] // pieces
    row_operands = []
    for task in tasks:
        if not any(task[0] is r for r in row_operands):
            row_operands.append(task[0])
    addends = [t[4] for t in tasks if t[4] is not None]
    out_shape, scratch, nbytes = [], [], 0
    for rows, _, _, width, addend in tasks:
        count, wide = rows.shape[1], picked * width
        shapes = [(count, wide)] if addend is None else [(count, width)] * picked
        out_shape += [jax.ShapeDtypeStruct(shape, jnp.bfloat16) for shape in shapes]
        scratch += [
            pltpu.VMEM((pieces, filled, wide), jnp.bfloat16),
            pltpu.VMEM((count, wide), jnp.float32),
            pltpu.SemaphoreType.DMA((pieces, picked)),
        ]
        nbytes += pieces * filled * wide * 2 + count * wide * 8
        if addend is not None:
            scratch += [pltpu.VMEM((count, wide), jnp.bfloat16), pltpu.SemaphoreType.DMA]
            nbytes += count * wide * 2
    nbytes += sum(r.size * 2 for r in row_operands)

    def kernel(starts_ref, weights_ref, *refs):
        refs = list(refs)

        def take(n):
            return [refs.pop(0) for _ in range(n)]

        row_refs, addend_refs = take(len(row_operands)), take(len(addends))
        if after is not None:
            take(1)
        outs, jobs = take(len(out_shape)), []
        for rows, which, first, width, addend in tasks:
            rows_ref = row_refs[next(i for i, r in enumerate(row_operands) if r is rows)]
            out_refs = [outs.pop(0) for _ in range(1 if addend is None else picked)]
            weights_here, total, weight_sems = take(3)
            wide = picked * width

            def copies(p, which=which, first=first, width=width, weights_here=weights_here, weight_sems=weight_sems):
                depths = pl.ds(pl.multiple_of(p * length, 16), length)
                found = []
                for i in range(picked):
                    begin = pl.multiple_of(starts_ref[which, i] + first, 128)
                    source = weights_ref.at[depths, pl.ds(begin, width)]
                    target = weights_here.at[p, pl.ds(0, length), pl.ds(i * width, width)]
                    found.append(pltpu.make_async_copy(source, target, weight_sems.at[p, i]))
                return found

            for p in range(pieces):
                for copy in copies(p):
                    copy.start()
            addend_copy = addend_here = None
            if addend is not None:
                addend_here, addend_sem = take(2)
                addend_copy = pltpu.make_async_copy(addend_refs.pop(0), addend_here, addend_sem)
                addend_copy.start()
            jobs.append((rows_ref, weights_here, total, copies, addend_copy, addend_here, out_refs, wide))
        for rows_ref, weights_here, total, copies, addend_copy, addend_here, out_refs, wide in jobs:
            for p in range(pieces):
                weights_here[p, length:, :] = jnp.zeros((filled - length, wide), jnp.bfloat16)
            total[...] = jnp.zeros_like(total)

            def step(p, carry, rows_ref=rows_ref, weights_here=weights_here, total=total, copies=copies):
                for copy in copies(p):
                    copy.wait()
                total[...] += dot(rows_ref[p], weights_here[p], ((1,), (0,)))
                return carry

            lax.fori_loop(0, pieces, step, 0)
            whole = total[...]
            if addend_copy is not None:
                addend_copy.wait()
                whole = whole + addend_here[...].astype(jnp.float32)
            for i, out_ref in enumerate(out_refs):
                out_ref[...] = whole[:, i * out_ref.shape[1] : (i + 1) * out_ref.shape[1]].astype(jnp.bfloat16)

    vmem, hbm = pl.BlockSpec(memory_space=pltpu.VMEM), pl.BlockSpec(memory_space=pl.ANY)
    extra = addends + ([after] if after is not None else [])
    return pl.pallas_call(
        kernel,
        in_specs=[pl.BlockSpec(memory_space=pltpu.SMEM), hbm] + [vmem] * len(row_operands) + [hbm] * len(extra),
        out_specs=[vmem] * len(out_shape),
        out_shape=out_shape,
        scratch_shapes=scratch,
        compiler_params=pltpu.CompilerParams(vmem_limit_bytes=nbytes + VMEM_SPARE),
        cost_estimate=pl.CostEstimate(flops=1 << 20, bytes_accessed=1 << 14, transcendentals=0),
    )(starts, weights, *row_operands, *extra)


def pack(picks, columns):
    held, count = picks[0].shape
    depth = columns[0].shape[0]
    pieces = next(n for n in range(1, depth) if depth % (16 * n) == 0 and depth // n <= PIECE)
    length = depth // pieces
    filled = -(-length // 128) * 128

    def kernel(*refs):
        out_ref = refs[-1]
        total = dot(refs[0][...], refs[len(picks)][...], ((1,), (1,)))
        out_ref[0, :, :length] = total.astype(jnp.bfloat16)
        for i in range(1, len(picks)):
            more = dot(refs[i][...], refs[len(picks) + i][...], ((1,), (1,)))
            height = more.shape[0]
            out_ref[0, :height, :length] = (total[:height] + more).astype(jnp.bfloat16)
        out_ref[0, :, length:] = jnp.zeros((held, filled - length), jnp.bfloat16)

    return pl.pallas_call(
        kernel,
        grid=(pieces,),
        in_specs=[pl.BlockSpec(pick.shape, lambda k: (0, 0)) for pick in picks]
        + [pl.BlockSpec((length, count), lambda k: (k, 0)) for _ in picks],
        out_specs=pl.BlockSpec((1, held, filled), lambda k: (k, 0, 0)),
        out_shape=jax.ShapeDtypeStruct((pieces, held, filled), jnp.bfloat16),
        compiler_params=pltpu.CompilerParams(vmem_limit_bytes=VMEM_LIMIT),
        cost_estimate=pl.CostEstimate(flops=1 << 20, bytes_accessed=1 << 14, transcendentals=0),
    )(*picks, *columns)


class Grid:
    def __init__(self):
        self.core = lax.axis_index("dp")
        tp = lax.axis_index("tp")
        self.y = tp % 2
        self.u = jnp.where(self.core == 0, tp // 2, 3 - tp // 2)

    @staticmethod
    def at(core, u, y):
        return core * 8 + (u if core == 0 else 3 - u) * 2 + y

    def send(self, value, move):
        pairs = []
        for core in range(2):
            for u in range(4):
                for y in range(2):
                    to = move(core, u, y)
                    if to is not None:
                        pairs.append((self.at(core, u, y), self.at(*to)))
        return lax.ppermute(value, ("dp", "tp"), pairs)

    def across(self, value):
        return self.send(value, lambda c, u, y: (c, u, 1 - y))

    def along(self, value, ends, idle):
        return self.send(value, lambda c, u, y: (c, ends[u], y) if u in ends else idle(c, u, y))

    @staticmethod
    def stay(c, u, y):
        return c, u, y

    @staticmethod
    def other_core(c, u, y):
        return 1 - c, 3 - u, y

    def to_other_core(self, value):
        return self.send(value, self.other_core)

    def blocks(self, y, tp_width):
        starts = []
        for k in range(2):
            u = (self.u + k) % 2
            starts.append((jnp.where(self.core == 0, u, 1 - u) * 2 + y) * tp_width)
        return jnp.stack(starts).astype(jnp.int32)


class Order:
    def __init__(self):
        self.mark = None

    def tie(self, value):
        if self.mark is None:
            return value
        return lax.optimization_barrier((value, self.mark))[0]


def f32(value):
    return value.astype(jnp.float32)


def pipeline(grid, order, weights, chunks, tp_width, beside):
    starts = jnp.stack([grid.blocks(1 - grid.y, tp_width), grid.blocks(grid.y, tp_width)])
    away, home = 0, 1
    count = len(chunks)
    state = [{} for _ in chunks]

    def sending(s):
        rows, first, width, _ = chunks[s]
        return rows(), away, first, width, None

    def sent(s, value):
        state[s]["across"] = grid.across(value)

    for s in range(2):
        task = sending(s)
        (value,) = project(weights, order.tie(starts), [task], order.mark)
        order.mark = value
        sent(s, value)
        if s - 2 in beside:
            order.mark = beside[s - 2](order)
    for s in range(count + 1):
        if s < count:
            rows, first, width, _ = chunks[s]
            tasks = [sending(s + 2)] if s + 2 < count else []
            tasks.append((rows(), home, first, width, state[s]["across"]))
            *values, same, other = project(weights, order.tie(starts), tasks, order.mark)
            order.mark = other
            if values:
                sent(s + 2, values[0])
            state[s]["parts"] = [
                same,
                grid.along(same, {3: 1, 2: 0}, grid.other_core),
                grid.along(other, {3: 0, 2: 1}, grid.other_core),
                grid.along(other, {1: 0, 0: 1}, grid.stay),
            ]
        if s in beside:
            order.mark = beside[s](order)
        if s > 0:
            same, *others = state[s - 1]["parts"]
            total = f32(order.tie(same))
            for part in others:
                total = total + f32(part)
            state[s - 1]["sum"] = order.mark = total.astype(jnp.bfloat16)
            if chunks[s - 1][3]:
                state[s - 1]["moved"] = grid.to_other_core(state[s - 1]["sum"])
    return [c["sum"] for c in state], [c.get("moved") for c in state]


def low_rank_partial(layer_input_rows, columns, down, up, adapter_of):
    table, rank, _ = down.shape
    count = layer_input_rows.shape[0]
    down_all = dot(down.reshape(table * rank, -1), layer_input_rows, ((1,), (1,)))
    back_all = dot(up.reshape(table * rank, -1), columns, ((1,), (0,)))

    def pick(wide):
        return jnp.sum(jnp.where(adapter_of[:, None, :], wide.reshape(table, rank, count), 0.0), axis=0)

    return jnp.concatenate([pick(down_all), pick(back_all)], axis=0)


def low_rank_split(total, live):
    rank = total.shape[0] // 2
    total = jnp.where(live[None, :], total, 0.0).astype(jnp.bfloat16)
    return total[:rank], total[rank:]


def spread(low, chosen):
    rank, count = low.shape
    wide = jnp.where(chosen[:, None, :], low[None, :, :], jnp.zeros((), low.dtype))
    return wide.reshape(chosen.shape[0] * rank, count)


def owned_gradient(core, wide, values, contract, rank):
    total = ADAPTER_SCALE * dot(wide, values, ((1,), (contract,)))
    half = total.shape[0] // 2
    mine = lax.dynamic_slice_in_dim(total, core * half, half, 0)
    other = lax.dynamic_slice_in_dim(total, (1 - core) * half, half, 0)
    got = lax.ppermute(other.astype(jnp.bfloat16), "dp", [(0, 1), (1, 0)])
    return (mine + got.astype(jnp.float32)).reshape(half // rank, rank, -1)


def routing(row_adapter_index, counts, offsets, gradient_owner_slot):
    table = counts.shape[1]
    numbers = jnp.arange(table, dtype=jnp.int32)
    adapter_of = row_adapter_index[None, :] == numbers[:, None]
    ahead = jnp.sum(jnp.where(offsets[0][None, :] < offsets[0][:, None], counts[0][None, :], 0), axis=1)

    def of_row(values):
        return jnp.sum(jnp.where(adapter_of, values[:, None], 0), axis=0)

    slot_of = of_row(gradient_owner_slot)[None, :] == numbers[:, None]
    since = jnp.arange(row_adapter_index.shape[0], dtype=jnp.int32) - of_row(offsets[0] * BLOCK)
    live = (row_adapter_index < table) & (since >= 0) & (since < of_row(counts[0]))
    place = jnp.where(live, of_row(ahead) + since, -1)
    return adapter_of, slot_of, live, place


def seated(place, live, first, held):
    seats = first + jnp.arange(held, dtype=jnp.int32)
    return ((place[None, :] == seats[:, None]) & live[None, :]).astype(jnp.bfloat16)


def packed_step(capacity, held, args, route, theirs, low):
    layer_input_rows, columns, weights, adapter_down_matrices, adapter_up_matrices = args
    adapter_of, slot_of, live, place = route
    tp_width = layer_input_rows.shape[1]
    table, rank, _ = adapter_down_matrices.shape
    grid, order = Grid(), Order()
    alone = capacity - held
    cache = {"low": low[0], "got": low[1]}

    def own_rows():
        if "own" not in cache:
            cache["own"] = order.mark = pack([seated(place, live, 0, alone)], [columns])
        return cache["own"]

    def shared_rows():
        if "shared" not in cache:
            their_columns, their_place = theirs
            picks, from_columns = [seated(held - 1 - their_place, their_place >= 0, 0, held)], [their_columns]
            if held > alone:
                picks.append(seated(place, live, alone, held - alone))
                from_columns.append(columns)
            cache["shared"] = order.mark = pack(order.tie(picks), from_columns)
        return cache["shared"]

    def next_low_rank(bit):
        def run(order):
            cache["low"] = order.tie(cache["low"]) + cache["got"]
            if bit:
                cache["got"] = lax.ppermute(cache["low"], "tp", [(i, i ^ bit) for i in range(8)])
            return cache["low"]

        return run

    def gradients(order):
        low = next_low_rank(0)(order)
        reduced, back = low_rank_split(low, live)
        cache["back"] = back
        cache["up"] = owned_gradient(grid.core, spread(reduced, slot_of), columns, 1, rank)
        cache["down"] = owned_gradient(grid.core, spread(back, slot_of), layer_input_rows, 0, rank)
        return low

    own_cuts, shared_cuts = cuts_of(tp_width, OWN_CUTS), cuts_of(tp_width, SHARED_CUTS)
    chunks = [(own_rows, f, w, False) for f, w in own_cuts] + [
        (shared_rows, f, w, True) for f, w in shared_cuts
    ]
    beside = {-2: next_low_rank(2), 0: next_low_rank(4), 1: gradients}
    sums, moved = pipeline(grid, order, weights, chunks, tp_width, beside)
    first = len(own_cuts)
    kept = jnp.concatenate(sums[:first], axis=1)
    if held > alone:
        rest = jnp.concatenate([c[: held - alone] for c in sums[first:]], axis=1)
        kept = jnp.concatenate([kept, rest], axis=0)
    arrived = jnp.where(grid.u < 2, kept, jnp.concatenate(moved[first:], axis=1))
    pick = seated(jnp.where(grid.u < 2, place, held - 1 - place), live, 0, held)
    base = dot(pick, arrived, ((0,), (0,)))
    contribution = dot(
        spread(cache["back"], adapter_of), adapter_down_matrices.reshape(table * rank, -1), ((0,), (0,))
    )
    input_gradient = jnp.where(live[:, None], base + ADAPTER_SCALE * contribution, 0.0).astype(jnp.bfloat16)
    return input_gradient, cache["down"], cache["up"]


def rotation(groups, k, d):
    return [(2 * g + c, (g + k) % groups * 2 + (c + d) % 2) for g in range(groups) for c in range(2)]


def cuts_of(width, eighths):
    cuts, first = [], 0
    for part in eighths:
        cuts.append((first, width * part // 8))
        first += width * part // 8
    return cuts


def grid_body(
    layer_input_rows,
    cotangent,
    frozen_up_matrix,
    adapter_down_matrices,
    adapter_up_matrices,
    row_adapter_index,
    counts,
    offsets,
    gradient_owner_slot,
):
    count = layer_input_rows.shape[0]
    mine = jnp.sum(counts)
    here = jnp.stack([mine, mine]).reshape(2, 1)
    groups = lax.axis_size("dom")
    found = [lax.ppermute(here, ("dom", "dp"), rotation(groups, k, d)) for k in range(groups) for d in range(2) if k + d]
    totals = [here[0, 0]] + [f[0, 0] for f in found]
    most = functools.reduce(jnp.maximum, totals)
    both = functools.reduce(jnp.maximum, [totals[2 * k] + totals[2 * k + 1] for k in range(groups)])
    route = routing(row_adapter_index, counts, offsets, gradient_owner_slot)
    args = (layer_input_rows, cotangent.T, frozen_up_matrix.T, adapter_down_matrices, adapter_up_matrices)
    theirs = tuple(lax.ppermute(v, "dp", [(0, 1), (1, 0)]) for v in (args[1], route[3]))
    low = low_rank_partial(layer_input_rows, args[1], adapter_down_matrices, adapter_up_matrices, route[0])
    low = low, lax.ppermute(low, "tp", [(i, i ^ 1) for i in range(8)])
    sizes = [(count * c // 12, count * h // 12) for c, h in SIZES]
    branch = jnp.zeros((), jnp.int32)
    for capacity, held in sizes[:-1]:
        branch = branch + ((both > capacity) | (most > held)).astype(jnp.int32)
    steps = [functools.partial(packed_step, *size) for size in sizes]
    if len(steps) == 1:
        return steps[0](args, route, theirs, low)
    return lax.switch(branch, steps, args, route, theirs, low)


def general_body(
    layer_input_rows,
    cotangent,
    frozen_up_matrix,
    adapter_down_matrices,
    adapter_up_matrices,
    row_adapter_index,
    counts,
    offsets,
    gradient_owner_slot,
):
    table, rank, _ = adapter_down_matrices.shape
    core = lax.axis_index("dp")
    adapter_of, slot_of, live, _ = routing(row_adapter_index, counts, offsets, gradient_owner_slot)
    partial = low_rank_partial(
        layer_input_rows, cotangent.T, adapter_down_matrices, adapter_up_matrices, adapter_of
    )
    reduced, back = low_rank_split(lax.psum(partial, "tp"), live)
    weights = lax.all_gather(frozen_up_matrix, "dp", axis=0, tiled=True)
    partial = dot(cotangent, weights, ((1,), (1,))).astype(jnp.bfloat16)
    base = lax.psum_scatter(partial, "tp", scatter_dimension=1, tiled=True).astype(jnp.float32)
    owned_up = owned_gradient(core, spread(reduced, slot_of), cotangent.T, 1, rank)
    owned_down = owned_gradient(core, spread(back, slot_of), layer_input_rows, 0, rank)
    contribution = dot(
        spread(back, adapter_of), adapter_down_matrices.reshape(table * rank, -1), ((0,), (0,))
    )
    input_gradient = jnp.where(live[:, None], base + ADAPTER_SCALE * contribution, 0.0).astype(jnp.bfloat16)
    return input_gradient, owned_down, owned_up


def solution(mesh):
    in_specs = (
        P(("dom", "dp"), "tp"),
        P(("dom", "dp"), "tp"),
        P("dp", "tp"),
        P("dom", None, "tp"),
        P("dom", None, "tp"),
        P(("dom", "dp")),
        P(("dom", "dp"), None),
        P(("dom", "dp"), None),
        P("dom"),
    )
    out_specs = (P(("dom", "dp"), "tp"), P(("dom", "dp"), None, "tp"), P(("dom", "dp"), None, "tp"))
    body = grid_body if mesh.shape["tp"] == 8 and mesh.shape["dp"] == 2 else general_body
    return jax.shard_map(body, mesh=mesh, in_specs=in_specs, out_specs=out_specs, check_vma=False)
```

```python
import functools

import jax
import jax.numpy as jnp
from jax import lax
from jax.experimental import pallas as pl
from jax.experimental.pallas import tpu as pltpu
from jax.sharding import PartitionSpec as P

BLOCK = 128
ADAPTER_SCALE = 0.5
VMEM_LIMIT = 36 << 20
PACK_LIMIT = 56 << 20
VMEM_SPARE = 4 << 20
HIDE = 4
PIECE = 1280
SIZES = ((18, 11), (24, 12))
OWN_CUTS = (4, 4)
SHARED_CUTS = (3, 3, 2)


def dot(a, b, dims):
    return lax.dot_general(a, b, (dims, ((), ())), preferred_element_type=jnp.float32)


def project(weights, starts, tasks, after=None):
    picked = starts.shape[1]
    pieces, _, filled = tasks[0][0].shape
    length = weights.shape[0] // pieces
    row_operands = []
    for task in tasks:
        if not any(task[0] is r for r in row_operands):
            row_operands.append(task[0])
    addends = [t[4][0] for t in tasks if t[4] is not None]
    out_shape, scratch, nbytes = [], [], 0
    for rows, _, _, width, addend in tasks:
        count, wide = rows.shape[1], picked * width
        shapes = [(count, wide)] if addend is None else [(count, width)] * picked
        out_shape += [jax.ShapeDtypeStruct(shape, jnp.bfloat16) for shape in shapes]
        scratch += [
            pltpu.VMEM((pieces, filled, wide), jnp.bfloat16),
            pltpu.VMEM((count, wide), jnp.float32),
            pltpu.SemaphoreType.DMA((pieces, picked)),
        ]
        nbytes += pieces * filled * wide * 2 + count * wide * 4
        if addend is not None:
            scratch += [pltpu.VMEM((count, wide), jnp.bfloat16), pltpu.SemaphoreType.DMA((picked,))]
            nbytes += count * wide * 2
    flops = HIDE * sum(2 * t[0].shape[1] * weights.shape[0] * picked * t[3] for t in tasks) if addends else 1 << 20

    def kernel(starts_ref, weights_ref, *refs):
        refs = list(refs)

        def take(n):
            return [refs.pop(0) for _ in range(n)]

        row_refs, addend_refs = take(len(row_operands)), take(len(addends))
        if after is not None:
            take(1)
        outs, jobs = take(len(out_shape)), []
        for rows, which, first, width, addend in tasks:
            rows_ref = row_refs[next(i for i, r in enumerate(row_operands) if r is rows)]
            out_refs = [outs.pop(0) for _ in range(1 if addend is None else picked)]
            weights_here, total, weight_sems = take(3)
            wide = picked * width

            def copies(p, which=which, first=first, width=width, weights_here=weights_here, weight_sems=weight_sems):
                depths = pl.ds(pl.multiple_of(p * length, 16), length)
                found = []
                for i in range(picked):
                    begin = pl.multiple_of(starts_ref[which, i] + first, 128)
                    source = weights_ref.at[depths, pl.ds(begin, width)]
                    target = weights_here.at[p, pl.ds(0, length), pl.ds(i * width, width)]
                    found.append(pltpu.make_async_copy(source, target, weight_sems.at[p, i]))
                return found

            for p in range(pieces):
                for copy in copies(p):
                    copy.start()
            addend_copies, addend_here = [], None
            if addend is not None:
                addend_here, addend_sems = take(2)
                addend_ref = addend_refs.pop(0)
                for i in range(picked):
                    source = addend_ref.at[:, pl.ds(i * (addend[0].shape[1] // picked) + addend[1], width)]
                    target = addend_here.at[:, pl.ds(i * width, width)]
                    addend_copies.append(pltpu.make_async_copy(source, target, addend_sems.at[i]))
                    addend_copies[i].start()
            jobs.append((rows_ref, weights_here, total, copies, addend_copies, addend_here, out_refs, wide))
        for rows_ref, weights_here, total, copies, addend_copies, addend_here, out_refs, wide in jobs:
            for p in range(pieces):
                weights_here[p, length:, :] = jnp.zeros((filled - length, wide), jnp.bfloat16)
            total[...] = jnp.zeros_like(total)

            def step(p, carry, rows_ref=rows_ref, weights_here=weights_here, total=total, copies=copies):
                for copy in copies(p):
                    copy.wait()
                total[...] += dot(rows_ref[p], weights_here[p], ((1,), (0,)))
                return carry

            lax.fori_loop(0, pieces, step, 0)
            whole = total[...]
            for copy in addend_copies:
                copy.wait()
            if addend_copies:
                whole = whole + addend_here[...].astype(jnp.float32)
            for i, out_ref in enumerate(out_refs):
                out_ref[...] = whole[:, i * out_ref.shape[1] : (i + 1) * out_ref.shape[1]].astype(jnp.bfloat16)

    vmem, anywhere = pl.BlockSpec(memory_space=pltpu.VMEM), pl.BlockSpec(memory_space=pl.ANY)
    hbm = pl.BlockSpec(memory_space=pltpu.HBM)
    extra = addends + ([after] if after is not None else [])
    return pl.pallas_call(
        kernel,
        in_specs=[pl.BlockSpec(memory_space=pltpu.SMEM), hbm] + [vmem] * len(row_operands) + [anywhere] * len(extra),
        out_specs=[vmem] * len(out_shape),
        out_shape=out_shape,
        scratch_shapes=scratch,
        compiler_params=pltpu.CompilerParams(vmem_limit_bytes=max(nbytes + VMEM_SPARE, VMEM_LIMIT)),
        cost_estimate=pl.CostEstimate(flops=flops, bytes_accessed=1 << 14, transcendentals=0),
    )(starts, weights, *row_operands, *extra)


def pack(seats, columns):
    held, count = seats[0][1], seats[0][0].shape[0]
    depth = columns[0].shape[0]
    pieces = next(n for n in range(1, depth) if depth % (16 * n) == 0 and depth // n <= PIECE)
    length = depth // pieces
    filled = -(-length // 128) * 128
    heights = [height for _, height in seats]

    def kernel(*refs):
        seat_refs, refs = refs[: len(seats)], refs[len(seats) :]
        column_refs, (out_ref, *picks) = refs[: len(seats)], refs[len(seats) :]

        @pl.when(pl.program_id(0) == 0)
        def _():
            for seat_ref, pick_ref in zip(seat_refs, picks):
                number = lax.broadcasted_iota(jnp.int32, pick_ref.shape, 0)
                pick_ref[...] = jnp.where(number == seat_ref[...], 1.0, 0.0).astype(jnp.bfloat16)

        total = dot(picks[0][...], column_refs[0][...], ((1,), (1,)))
        out_ref[0, :, :length] = total.astype(jnp.bfloat16)
        for i in range(1, len(seats)):
            more = dot(picks[i][...], column_refs[i][...], ((1,), (1,)))
            out_ref[0, : heights[i], :length] = (total[: heights[i]] + more).astype(jnp.bfloat16)
        out_ref[0, :, length:] = jnp.zeros((held, filled - length), jnp.bfloat16)

    return pl.pallas_call(
        kernel,
        grid=(pieces,),
        in_specs=[pl.BlockSpec((1, count), lambda k: (0, 0)) for _ in seats]
        + [pl.BlockSpec((length, count), lambda k: (k, 0)) for _ in seats],
        out_specs=pl.BlockSpec((1, held, filled), lambda k: (k, 0, 0)),
        out_shape=jax.ShapeDtypeStruct((pieces, held, filled), jnp.bfloat16),
        scratch_shapes=[pltpu.VMEM((height, count), jnp.bfloat16) for height in heights],
        compiler_params=pltpu.CompilerParams(vmem_limit_bytes=PACK_LIMIT),
        cost_estimate=pl.CostEstimate(flops=1 << 20, bytes_accessed=1 << 14, transcendentals=0),
    )(*[seat[None, :] for seat, _ in seats], *columns)


class Grid:
    def __init__(self):
        self.core = lax.axis_index("dp")
        tp = lax.axis_index("tp")
        self.y = tp % 2
        self.u = jnp.where(self.core == 0, tp // 2, 3 - tp // 2)

    @staticmethod
    def at(core, u, y):
        return core * 8 + (u if core == 0 else 3 - u) * 2 + y

    def send(self, value, move):
        pairs = []
        for core in range(2):
            for u in range(4):
                for y in range(2):
                    to = move(core, u, y)
                    if to is not None:
                        pairs.append((self.at(core, u, y), self.at(*to)))
        return lax.ppermute(value, ("dp", "tp"), pairs)

    def across(self, value):
        return self.send(value, lambda c, u, y: (c, u, 1 - y))

    def along(self, value, ends, idle):
        return self.send(value, lambda c, u, y: (c, ends[u], y) if u in ends else idle(c, u, y))

    @staticmethod
    def none(c, u, y):
        return None

    @staticmethod
    def other_core(c, u, y):
        return 1 - c, 3 - u, y

    def to_other_core(self, value):
        return self.send(value, self.other_core)

    def blocks(self, y, tp_width):
        starts = []
        for k in range(2):
            u = (self.u + k) % 2
            starts.append((jnp.where(self.core == 0, u, 1 - u) * 2 + y) * tp_width)
        return jnp.stack(starts).astype(jnp.int32)


class Order:
    def __init__(self):
        self.mark = None

    def tie(self, value):
        if self.mark is None:
            return value
        return lax.optimization_barrier((value, self.mark))[0]


def f32(value):
    return value.astype(jnp.float32)


class Chunks:
    def __init__(self, grid, order, weights, tp_width):
        self.grid, self.order, self.weights = grid, order, weights
        self.starts = jnp.stack([grid.blocks(1 - grid.y, tp_width), grid.blocks(grid.y, tp_width)])

    def run(self, to_send=(), to_keep=None, done=()):
        tasks = [(k["rows"], 0, k["first"], k["width"], None) for k in to_send]
        if to_keep is not None:
            tasks.append((to_keep["rows"], 1, to_keep["first"], to_keep["width"], to_keep["across"]))
        values = project(self.weights, self.order.tie(self.starts), tasks, self.order.mark)
        values, done = lax.optimization_barrier((values, tuple(done)))
        self.order.mark = values[-1]
        for chunk, value in zip(to_send, values):
            chunk["product"] = value
        if to_keep is not None:
            to_keep["same"], to_keep["other"] = values[-2:]
        return done

    def across(self, chunk):
        chunk["across"] = (self.grid.across(chunk["product"]), 0)

    def along(self, chunk):
        grid, same, other = self.grid, chunk["same"], chunk["other"]
        chunk["parts"] = (
            grid.along(same, {3: 1, 2: 0}, grid.other_core),
            grid.along(other, {3: 0, 2: 1}, grid.other_core),
            grid.along(other, {1: 0, 0: 1}, grid.none),
        )

    def finish(self, chunk, moved):
        total = f32(self.order.tie(chunk["same"]))
        for part in chunk["parts"]:
            total = total + f32(part)
        chunk["sum"] = self.order.mark = total.astype(jnp.bfloat16)
        if moved:
            chunk["moved"] = self.grid.to_other_core(chunk["sum"])


def low_rank_partial(layer_input_rows, columns, down, up, adapter_of):
    table, rank, _ = down.shape
    count = layer_input_rows.shape[0]
    down_all = dot(down.reshape(table * rank, -1), layer_input_rows, ((1,), (1,)))
    back_all = dot(up.reshape(table * rank, -1), columns, ((1,), (0,)))

    def pick(wide):
        return jnp.sum(jnp.where(adapter_of[:, None, :], wide.reshape(table, rank, count), 0.0), axis=0)

    return jnp.concatenate([pick(down_all), pick(back_all)], axis=0)


def low_rank_split(total, live):
    rank = total.shape[0] // 2
    total = jnp.where(live[None, :], total, 0.0).astype(jnp.bfloat16)
    return total[:rank], total[rank:]


def spread(low, chosen):
    rank, count = low.shape
    wide = jnp.where(chosen[:, None, :], low[None, :, :], jnp.zeros((), low.dtype))
    return wide.reshape(chosen.shape[0] * rank, count)


def owned_gradients(core, pairs):
    totals = [ADAPTER_SCALE * dot(wide, values, ((1,), (contract,))) for wide, values, contract in pairs]
    half = totals[0].shape[0] // 2

    def part(total, which):
        return lax.dynamic_slice_in_dim(total, which * half, half, 0)

    other = jnp.concatenate([part(t, 1 - core).astype(jnp.bfloat16) for t in totals], axis=1)
    got = lax.ppermute(other, "dp", [(0, 1), (1, 0)])
    mine = jnp.concatenate([part(t, core) for t in totals], axis=1)
    return mine, got


def split_gradients(mine, got, pairs, rank):
    total = mine + f32(got)
    half, first = total.shape[0], 0
    owned = []
    for _, values, contract in pairs:
        width = values.shape[1 - contract]
        owned.append(total[:, first : first + width].reshape(half // rank, rank, width))
        first += width
    return owned


def rank_products(core, reduced, back, back_by_adapter, columns, values, down):
    width, depth = values.shape[1], columns.shape[0]
    half = reduced.shape[0] // 2

    def kernel(core_ref, reduced_ref, back_ref, by_adapter_ref, columns_ref, values_ref, down_ref, *outs):
        other_ref, mine_ref, row_ref = outs
        for out_ref, which in ((other_ref, 1 - core_ref[0]), (mine_ref, core_ref[0])):
            part = pl.ds(pl.multiple_of(which * half, 16), half)
            out_ref[:, :width] = (ADAPTER_SCALE * dot(back_ref[part], values_ref[...], ((1,), (0,)))).astype(out_ref.dtype)
            out_ref[:, width:] = (ADAPTER_SCALE * dot(reduced_ref[part], columns_ref[...], ((1,), (1,)))).astype(
                out_ref.dtype
            )
        row_ref[...] = dot(by_adapter_ref[...], down_ref[...], ((0,), (0,)))

    vmem = pl.BlockSpec(memory_space=pltpu.VMEM)
    return pl.pallas_call(
        kernel,
        in_specs=[pl.BlockSpec(memory_space=pltpu.SMEM)] + [vmem] * 6,
        out_specs=[vmem] * 3,
        out_shape=[
            jax.ShapeDtypeStruct((half, width + depth), jnp.bfloat16),
            jax.ShapeDtypeStruct((half, width + depth), jnp.float32),
            jax.ShapeDtypeStruct(values.shape, jnp.float32),
        ],
        compiler_params=pltpu.CompilerParams(vmem_limit_bytes=VMEM_LIMIT),
        cost_estimate=pl.CostEstimate(flops=1 << 20, bytes_accessed=1 << 14, transcendentals=0),
    )(core.astype(jnp.int32)[None], reduced, back, back_by_adapter, columns, values, down)


def routing(row_adapter_index, counts, offsets, gradient_owner_slot):
    table = counts.shape[1]
    numbers = jnp.arange(table, dtype=jnp.int32)
    adapter_of = row_adapter_index[None, :] == numbers[:, None]
    ahead = jnp.sum(jnp.where(offsets[0][None, :] < offsets[0][:, None], counts[0][None, :], 0), axis=1)

    def of_row(values):
        return jnp.sum(jnp.where(adapter_of, values[:, None], 0), axis=0)

    slot_of = of_row(gradient_owner_slot)[None, :] == numbers[:, None]
    since = jnp.arange(row_adapter_index.shape[0], dtype=jnp.int32) - of_row(offsets[0] * BLOCK)
    live = (row_adapter_index < table) & (since >= 0) & (since < of_row(counts[0]))
    place = jnp.where(live, of_row(ahead) + since, -1)
    return adapter_of, slot_of, live, place


def seated(place, live, first, held):
    seats = first + jnp.arange(held, dtype=jnp.int32)
    return ((place[None, :] == seats[:, None]) & live[None, :]).astype(jnp.bfloat16)


def packed_step(capacity, held, args, route, theirs, low, own):
    layer_input_rows, columns, weights, adapter_down_matrices, adapter_up_matrices = args
    adapter_of, slot_of, live, place = route
    tp_width = layer_input_rows.shape[1]
    table, rank, _ = adapter_down_matrices.shape
    grid, order = Grid(), Order()
    chunks = Chunks(grid, order, weights, tp_width)
    alone = capacity - held
    if own.shape[1] != alone:
        own = pack([(place, alone)], [columns])

    def cut(part, parts, rows):
        return {"rows": rows, "first": tp_width * sum(parts[:part]) // 8, "width": tp_width * parts[part] // 8}

    a, b = (cut(i, OWN_CUTS, own) for i in range(2))
    chunks.run([a])
    chunks.across(a)
    low = low[0] + low[1]
    got = lax.ppermute(low, "tp", [(i, i ^ 2) for i in range(8)])
    their_columns, their_place = theirs
    seats, from_columns = [(jnp.where(their_place >= 0, held - 1 - their_place, -1), held)], [their_columns]
    if held > alone:
        seats.append((place - alone, held - alone))
        from_columns.append(columns)
    seats[0] = (order.tie(seats[0][0]), held)
    shared = order.mark = pack(seats, from_columns)
    c, d, e = (cut(i, SHARED_CUTS, shared) for i in range(3))
    (got,) = chunks.run([c], done=[got])
    chunks.across(c)
    low = low + got
    got = lax.ppermute(low, "tp", [(i, i ^ 4) for i in range(8)])
    (got,) = chunks.run([d], a, [got])
    low = low + got
    chunks.across(d)
    chunks.along(a)
    (a["parts"],) = chunks.run([b], c, [a["parts"]])
    chunks.across(b)
    chunks.along(c)
    chunks.run([e])
    chunks.finish(a, False)
    chunks.across(e)
    (c["parts"],) = chunks.run(to_keep=d, done=[c["parts"]])
    chunks.along(d)
    chunks.finish(c, True)
    low = order.tie(low)
    reduced, back = low_rank_split(low, live)
    other, mine, contribution = rank_products(
        grid.core,
        spread(reduced, slot_of),
        spread(back, slot_of),
        spread(back, adapter_of),
        columns,
        layer_input_rows,
        adapter_down_matrices.reshape(table * rank, -1),
    )
    order.mark = contribution
    got = lax.ppermute(other, "dp", [(0, 1), (1, 0)])
    (d["parts"],) = chunks.run(to_keep=b, done=[d["parts"]])
    chunks.along(b)
    chunks.finish(d, True)
    b["parts"], got = chunks.run(to_keep=e, done=[b["parts"], got])
    chunks.along(e)
    chunks.finish(b, False)
    owned = (order.tie(mine) + f32(got)).reshape(table // 2, rank, -1)
    owned_down, owned_up = owned[..., :tp_width], owned[..., tp_width:]
    order.mark = owned_down
    chunks.finish(e, True)

    kept = jnp.concatenate([a["sum"], b["sum"]], axis=1)
    if held > alone:
        rest = jnp.concatenate([k["sum"][: held - alone] for k in (c, d, e)], axis=1)
        kept = jnp.concatenate([kept, rest], axis=0)
    arrived = jnp.where(grid.u < 2, kept, jnp.concatenate([k["moved"] for k in (c, d, e)], axis=1))
    pick = seated(jnp.where(grid.u < 2, place, held - 1 - place), live, 0, held)
    base = dot(pick, arrived, ((0,), (0,)))
    input_gradient = jnp.where(live[:, None], base + ADAPTER_SCALE * contribution, 0.0).astype(jnp.bfloat16)
    return input_gradient, owned_down, owned_up


def rotation(groups, k, d):
    return [(2 * g + c, (g + k) % groups * 2 + (c + d) % 2) for g in range(groups) for c in range(2)]


def grid_body(
    layer_input_rows,
    cotangent,
    frozen_up_matrix,
    adapter_down_matrices,
    adapter_up_matrices,
    row_adapter_index,
    counts,
    offsets,
    gradient_owner_slot,
):
    count = layer_input_rows.shape[0]
    mine = jnp.sum(counts)
    here = jnp.stack([mine, mine]).reshape(2, 1)
    groups = lax.axis_size("dom")
    found = [lax.ppermute(here, ("dom", "dp"), rotation(groups, k, d)) for k in range(1, groups) for d in range(2)]
    args = (layer_input_rows, cotangent.T, frozen_up_matrix.T, adapter_down_matrices, adapter_up_matrices)
    sizes = [(count * c // 12, count * h // 12) for c, h in SIZES]
    row_adapter_index, _ = lax.optimization_barrier((row_adapter_index, here))
    route = routing(row_adapter_index, counts, offsets, gradient_owner_slot)
    theirs = tuple(lax.ppermute(v, "dp", [(0, 1), (1, 0)]) for v in (args[1], route[3]))
    low = low_rank_partial(layer_input_rows, args[1], adapter_down_matrices, adapter_up_matrices, route[0])
    low = low, lax.ppermute(low, "tp", [(i, i ^ 1) for i in range(8)])
    own = pack([(route[3], sizes[0][0] - sizes[0][1])], [args[1]])
    totals = [mine, jnp.max(theirs[1]) + 1] + [f[0, 0] for f in found]
    most = functools.reduce(jnp.maximum, totals)
    both = functools.reduce(jnp.maximum, [totals[2 * k] + totals[2 * k + 1] for k in range(groups)])
    branch = jnp.zeros((), jnp.int32)
    for capacity, held in sizes[:-1]:
        branch = branch + ((both > capacity) | (most > held)).astype(jnp.int32)
    steps = [functools.partial(packed_step, *size) for size in sizes]
    if len(steps) == 1:
        return steps[0](args, route, theirs, low, own)
    return lax.switch(branch, steps, args, route, theirs, low, own)


def general_body(
    layer_input_rows,
    cotangent,
    frozen_up_matrix,
    adapter_down_matrices,
    adapter_up_matrices,
    row_adapter_index,
    counts,
    offsets,
    gradient_owner_slot,
):
    table, rank, _ = adapter_down_matrices.shape
    core = lax.axis_index("dp")
    adapter_of, slot_of, live, _ = routing(row_adapter_index, counts, offsets, gradient_owner_slot)
    partial = low_rank_partial(
        layer_input_rows, cotangent.T, adapter_down_matrices, adapter_up_matrices, adapter_of
    )
    reduced, back = low_rank_split(lax.psum(partial, "tp"), live)
    weights = lax.all_gather(frozen_up_matrix, "dp", axis=0, tiled=True)
    partial = dot(cotangent, weights, ((1,), (1,))).astype(jnp.bfloat16)
    base = lax.psum_scatter(partial, "tp", scatter_dimension=1, tiled=True).astype(jnp.float32)
    pairs = [(spread(reduced, slot_of), cotangent.T, 1), (spread(back, slot_of), layer_input_rows, 0)]
    owned_up, owned_down = split_gradients(*owned_gradients(core, pairs), pairs, rank)
    contribution = dot(
        spread(back, adapter_of), adapter_down_matrices.reshape(table * rank, -1), ((0,), (0,))
    )
    input_gradient = jnp.where(live[:, None], base + ADAPTER_SCALE * contribution, 0.0).astype(jnp.bfloat16)
    return input_gradient, owned_down, owned_up


def solution(mesh):
    in_specs = (
        P(("dom", "dp"), "tp"),
        P(("dom", "dp"), "tp"),
        P("dp", "tp"),
        P("dom", None, "tp"),
        P("dom", None, "tp"),
        P(("dom", "dp")),
        P(("dom", "dp"), None),
        P(("dom", "dp"), None),
        P("dom"),
    )
    out_specs = (P(("dom", "dp"), "tp"), P(("dom", "dp"), None, "tp"), P(("dom", "dp"), None, "tp"))
    body = grid_body if mesh.shape["tp"] == 8 and mesh.shape["dp"] == 2 else general_body
    return jax.shard_map(body, mesh=mesh, in_specs=in_specs, out_specs=out_specs, check_vma=False)
```

```python
import functools

import jax
import jax.numpy as jnp
from jax import lax
from jax.experimental import pallas as pl
from jax.experimental.pallas import tpu as pltpu
from jax.sharding import PartitionSpec as P

BLOCK = 128
ADAPTER_SCALE = 0.5
VMEM_LIMIT = 36 << 20
PACK_LIMIT = 56 << 20
VMEM_SPARE = 4 << 20
HIDE = 2 * 10**9
PIECE = 1280
SIZES = ((18, 11, 4096), (24, 12, 256))
OWN_CUTS = (4, 4)
SHARED_CUTS = (3, 3, 2)


def dot(a, b, dims):
    return lax.dot_general(a, b, (dims, ((), ())), preferred_element_type=jnp.float32)


def project(weights, starts, tasks, after=None, most=512, flops=0):
    picked = starts.shape[1]
    pieces, _, filled = tasks[0][0].shape
    length = weights.shape[0] // pieces
    row_operands = []
    for task in tasks:
        if not any(task[0] is r for r in row_operands):
            row_operands.append(task[0])
    addends = [t[4][0] for t in tasks if t[4] is not None]
    out_shape, scratch, nbytes = [], [], 0
    for rows, _, _, width, addend in tasks:
        count, wide = rows.shape[1], picked * width
        shapes = [(count, wide)] if addend is None else [(count, width)] * picked
        out_shape += [jax.ShapeDtypeStruct(shape, jnp.bfloat16) for shape in shapes]
        scratch += [
            pltpu.VMEM((pieces, filled, wide), jnp.bfloat16),
            pltpu.VMEM((count, wide), jnp.float32),
            pltpu.SemaphoreType.DMA((pieces, picked)),
        ]
        nbytes += pieces * filled * wide * 2 + count * wide * 4
        if addend is not None:
            scratch += [pltpu.VMEM((count, wide), jnp.bfloat16), pltpu.SemaphoreType.DMA((picked,))]
            nbytes += count * wide * 2

    def kernel(starts_ref, weights_ref, *refs):
        refs = list(refs)

        def take(n):
            return [refs.pop(0) for _ in range(n)]

        row_refs, addend_refs = take(len(row_operands)), take(len(addends))
        if after is not None:
            take(1)
        outs, jobs = take(len(out_shape)), []
        for rows, which, first, width, addend in tasks:
            rows_ref = row_refs[next(i for i, r in enumerate(row_operands) if r is rows)]
            out_refs = [outs.pop(0) for _ in range(1 if addend is None else picked)]
            weights_here, total, weight_sems = take(3)
            wide = picked * width

            def copies(p, which=which, first=first, width=width, weights_here=weights_here, weight_sems=weight_sems):
                depths = pl.ds(pl.multiple_of(p * length, 16), length)
                found = []
                for i in range(picked):
                    begin = pl.multiple_of(starts_ref[which, i] + first, 128)
                    source = weights_ref.at[depths, pl.ds(begin, width)]
                    target = weights_here.at[p, pl.ds(0, length), pl.ds(i * width, width)]
                    found.append(pltpu.make_async_copy(source, target, weight_sems.at[p, i]))
                return found

            for p in range(pieces):
                for copy in copies(p):
                    copy.start()
            addend_copies, addend_here = [], None
            if addend is not None:
                addend_here, addend_sems = take(2)
                addend_ref = addend_refs.pop(0)
                for i in range(picked):
                    source = addend_ref.at[:, pl.ds(i * (addend[0].shape[1] // picked) + addend[1], width)]
                    target = addend_here.at[:, pl.ds(i * width, width)]
                    addend_copies.append(pltpu.make_async_copy(source, target, addend_sems.at[i]))
                    addend_copies[i].start()
            jobs.append((rows_ref, weights_here, total, copies, addend_copies, addend_here, out_refs, wide))
        for rows_ref, weights_here, total, copies, addend_copies, addend_here, out_refs, wide in jobs:
            for p in range(pieces):
                weights_here[p, length:, :] = jnp.zeros((filled - length, wide), jnp.bfloat16)
            total[...] = jnp.zeros_like(total)

            tile = next(t for t in range(min(most, wide), 0, -128) if wide % t == 0)

            def step(p, carry, rows_ref=rows_ref, weights_here=weights_here, total=total, copies=copies, tile=tile, wide=wide):
                for copy in copies(p):
                    copy.wait()

                def columns(j, carry):
                    part = pl.ds(pl.multiple_of(j * tile, 128), tile)
                    total[:, part] += dot(rows_ref[p], weights_here[p, :, part], ((1,), (0,)))
                    return carry

                return lax.fori_loop(0, wide // tile, columns, carry)

            lax.fori_loop(0, pieces, step, 0)
            whole = total[...]
            for copy in addend_copies:
                copy.wait()
            if addend_copies:
                whole = whole + addend_here[...].astype(jnp.float32)
            for i, out_ref in enumerate(out_refs):
                out_ref[...] = whole[:, i * out_ref.shape[1] : (i + 1) * out_ref.shape[1]].astype(jnp.bfloat16)

    vmem, anywhere = pl.BlockSpec(memory_space=pltpu.VMEM), pl.BlockSpec(memory_space=pl.ANY)
    hbm = pl.BlockSpec(memory_space=pltpu.HBM)
    extra = addends + ([after] if after is not None else [])
    return pl.pallas_call(
        kernel,
        in_specs=[pl.BlockSpec(memory_space=pltpu.SMEM), hbm] + [vmem] * len(row_operands) + [anywhere] * len(extra),
        out_specs=[vmem] * len(out_shape),
        out_shape=out_shape,
        scratch_shapes=scratch,
        compiler_params=pltpu.CompilerParams(vmem_limit_bytes=max(nbytes + VMEM_SPARE, VMEM_LIMIT)),
        cost_estimate=pl.CostEstimate(flops=flops, bytes_accessed=1 << 14, transcendentals=0),
    )(starts, weights, *row_operands, *extra)


def pack(seats, columns):
    held, count = seats[0][1], seats[0][0].shape[0]
    depth = columns[0].shape[0]
    pieces = next(n for n in range(1, depth) if depth % (16 * n) == 0 and depth // n <= PIECE)
    length = depth // pieces
    filled = -(-length // 128) * 128
    heights = [height for _, height in seats]

    def kernel(*refs):
        seat_refs, refs = refs[: len(seats)], refs[len(seats) :]
        column_refs, (out_ref, *picks) = refs[: len(seats)], refs[len(seats) :]

        @pl.when(pl.program_id(0) == 0)
        def _():
            for seat_ref, pick_ref in zip(seat_refs, picks):
                number = lax.broadcasted_iota(jnp.int32, pick_ref.shape, 0)
                pick_ref[...] = jnp.where(number == seat_ref[...], 1.0, 0.0).astype(jnp.bfloat16)

        total = dot(picks[0][...], column_refs[0][...], ((1,), (1,)))
        out_ref[0, :, :length] = total.astype(jnp.bfloat16)
        for i in range(1, len(seats)):
            more = dot(picks[i][...], column_refs[i][...], ((1,), (1,)))
            out_ref[0, : heights[i], :length] = (total[: heights[i]] + more).astype(jnp.bfloat16)
        out_ref[0, :, length:] = jnp.zeros((held, filled - length), jnp.bfloat16)

    return pl.pallas_call(
        kernel,
        grid=(pieces,),
        in_specs=[pl.BlockSpec((1, count), lambda k: (0, 0)) for _ in seats]
        + [pl.BlockSpec((length, count), lambda k: (k, 0)) for _ in seats],
        out_specs=pl.BlockSpec((1, held, filled), lambda k: (k, 0, 0)),
        out_shape=jax.ShapeDtypeStruct((pieces, held, filled), jnp.bfloat16),
        scratch_shapes=[pltpu.VMEM((height, count), jnp.bfloat16) for height in heights],
        compiler_params=pltpu.CompilerParams(vmem_limit_bytes=PACK_LIMIT),
        cost_estimate=pl.CostEstimate(flops=1 << 20, bytes_accessed=1 << 14, transcendentals=0),
    )(*[seat[None, :] for seat, _ in seats], *columns)


class Grid:
    def __init__(self):
        self.core = lax.axis_index("dp")
        tp = lax.axis_index("tp")
        self.y = tp % 2
        self.u = jnp.where(self.core == 0, tp // 2, 3 - tp // 2)

    @staticmethod
    def at(core, u, y):
        return core * 8 + (u if core == 0 else 3 - u) * 2 + y

    def send(self, value, move):
        pairs = []
        for core in range(2):
            for u in range(4):
                for y in range(2):
                    to = move(core, u, y)
                    if to is not None:
                        pairs.append((self.at(core, u, y), self.at(*to)))
        return lax.ppermute(value, ("dp", "tp"), pairs)

    def across(self, value):
        return self.send(value, lambda c, u, y: (c, u, 1 - y))

    def along(self, value, ends, idle):
        return self.send(value, lambda c, u, y: (c, ends[u], y) if u in ends else idle(c, u, y))

    @staticmethod
    def none(c, u, y):
        return None

    @staticmethod
    def other_core(c, u, y):
        return 1 - c, 3 - u, y

    def to_other_core(self, value):
        return self.send(value, self.other_core)

    def blocks(self, y, tp_width):
        starts = []
        for k in range(2):
            u = (self.u + k) % 2
            starts.append((jnp.where(self.core == 0, u, 1 - u) * 2 + y) * tp_width)
        return jnp.stack(starts).astype(jnp.int32)


class Order:
    def __init__(self):
        self.mark = None

    def tie(self, value):
        if self.mark is None:
            return value
        return lax.optimization_barrier((value, self.mark))[0]


def f32(value):
    return value.astype(jnp.float32)


class Chunks:
    def __init__(self, grid, order, weights, tp_width, tile):
        self.grid, self.order, self.weights, self.tile = grid, order, weights, tile
        self.starts = jnp.stack([grid.blocks(1 - grid.y, tp_width), grid.blocks(grid.y, tp_width)])

    def run(self, to_send=(), to_keep=None, done=(), flops=0):
        tasks = [(k["rows"], 0, k["first"], k["width"], None) for k in to_send]
        if to_keep is not None:
            across, column = to_keep["across"]
            tasks.append((to_keep["rows"], 1, to_keep["first"], to_keep["width"], (self.order.tie(across), column)))
        flops = flops or (HIDE if to_keep is not None else 1 << 20)
        values = project(self.weights, self.order.tie(self.starts), tasks, self.order.mark, self.tile, flops)
        values, done = lax.optimization_barrier((values, tuple(done)))
        self.order.mark = values[-1]
        for chunk, value in zip(to_send, values):
            chunk["product"] = value
        if to_keep is not None:
            to_keep["same"], to_keep["other"] = values[-2:]
        return done

    def across(self, chunk):
        chunk["across"] = (self.grid.across(chunk["product"]), 0)

    def along(self, chunk):
        grid, same, other = self.grid, chunk["same"], chunk["other"]
        chunk["parts"] = (
            grid.along(same, {3: 1, 2: 0}, grid.other_core),
            grid.along(other, {3: 0, 2: 1}, grid.other_core),
            grid.along(other, {1: 0, 0: 1}, grid.none),
        )

    def finish(self, chunk, moved):
        total = f32(self.order.tie(chunk["same"]))
        for part in chunk["parts"]:
            total = total + f32(part)
        chunk["sum"] = self.order.mark = total.astype(jnp.bfloat16)
        if moved:
            chunk["moved"] = self.grid.to_other_core(chunk["sum"])


def low_rank_partial(layer_input_rows, columns, down, up, adapter_of):
    table, rank, _ = down.shape
    count = layer_input_rows.shape[0]
    down_all = dot(down.reshape(table * rank, -1), layer_input_rows, ((1,), (1,)))
    back_all = dot(up.reshape(table * rank, -1), columns, ((1,), (0,)))

    def pick(wide):
        return jnp.sum(jnp.where(adapter_of[:, None, :], wide.reshape(table, rank, count), 0.0), axis=0)

    return jnp.concatenate([pick(down_all), pick(back_all)], axis=0)


def low_rank_split(total, live):
    rank = total.shape[0] // 2
    total = jnp.where(live[None, :], total, 0.0).astype(jnp.bfloat16)
    return total[:rank], total[rank:]


def spread(low, chosen):
    rank, count = low.shape
    wide = jnp.where(chosen[:, None, :], low[None, :, :], jnp.zeros((), low.dtype))
    return wide.reshape(chosen.shape[0] * rank, count)


def owned_gradients(core, pairs):
    totals = [ADAPTER_SCALE * dot(wide, values, ((1,), (contract,))) for wide, values, contract in pairs]
    half = totals[0].shape[0] // 2

    def part(total, which):
        return lax.dynamic_slice_in_dim(total, which * half, half, 0)

    other = jnp.concatenate([part(t, 1 - core).astype(jnp.bfloat16) for t in totals], axis=1)
    got = lax.ppermute(other, "dp", [(0, 1), (1, 0)])
    mine = jnp.concatenate([part(t, core) for t in totals], axis=1)
    return mine, got


def split_gradients(mine, got, pairs, rank):
    total = mine + f32(got)
    half, first = total.shape[0], 0
    owned = []
    for _, values, contract in pairs:
        width = values.shape[1 - contract]
        owned.append(total[:, first : first + width].reshape(half // rank, rank, width))
        first += width
    return owned


def rank_products(core, reduced, back, back_by_adapter, columns, values, down):
    width, depth = values.shape[1], columns.shape[0]
    half = reduced.shape[0] // 2

    def kernel(core_ref, reduced_ref, back_ref, by_adapter_ref, columns_ref, values_ref, down_ref, *outs):
        other_ref, mine_ref, row_ref = outs
        for out_ref, which in ((other_ref, 1 - core_ref[0]), (mine_ref, core_ref[0])):
            part = pl.ds(pl.multiple_of(which * half, 16), half)
            out_ref[:, :width] = (ADAPTER_SCALE * dot(back_ref[part], values_ref[...], ((1,), (0,)))).astype(out_ref.dtype)
            out_ref[:, width:] = (ADAPTER_SCALE * dot(reduced_ref[part], columns_ref[...], ((1,), (1,)))).astype(
                out_ref.dtype
            )
        row_ref[...] = dot(by_adapter_ref[...], down_ref[...], ((0,), (0,)))

    vmem = pl.BlockSpec(memory_space=pltpu.VMEM)
    return pl.pallas_call(
        kernel,
        in_specs=[pl.BlockSpec(memory_space=pltpu.SMEM)] + [vmem] * 6,
        out_specs=[vmem] * 3,
        out_shape=[
            jax.ShapeDtypeStruct((half, width + depth), jnp.bfloat16),
            jax.ShapeDtypeStruct((half, width + depth), jnp.float32),
            jax.ShapeDtypeStruct(values.shape, jnp.float32),
        ],
        compiler_params=pltpu.CompilerParams(vmem_limit_bytes=VMEM_LIMIT),
        cost_estimate=pl.CostEstimate(flops=1 << 20, bytes_accessed=1 << 14, transcendentals=0),
    )(core.astype(jnp.int32)[None], reduced, back, back_by_adapter, columns, values, down)


def routing(row_adapter_index, counts, offsets, gradient_owner_slot):
    table = counts.shape[1]
    numbers = jnp.arange(table, dtype=jnp.int32)
    adapter_of = row_adapter_index[None, :] == numbers[:, None]
    ahead = jnp.sum(jnp.where(offsets[0][None, :] < offsets[0][:, None], counts[0][None, :], 0), axis=1)

    def of_row(values):
        return jnp.sum(jnp.where(adapter_of, values[:, None], 0), axis=0)

    slot_of = of_row(gradient_owner_slot)[None, :] == numbers[:, None]
    since = jnp.arange(row_adapter_index.shape[0], dtype=jnp.int32) - of_row(offsets[0] * BLOCK)
    live = (row_adapter_index < table) & (since >= 0) & (since < of_row(counts[0]))
    place = jnp.where(live, of_row(ahead) + since, -1)
    return adapter_of, slot_of, live, place


def seated(place, live, first, held):
    seats = first + jnp.arange(held, dtype=jnp.int32)
    return ((place[None, :] == seats[:, None]) & live[None, :]).astype(jnp.bfloat16)


def packed_step(capacity, held, tile, args, route, theirs, low, own):
    layer_input_rows, columns, weights, adapter_down_matrices, adapter_up_matrices = args
    adapter_of, slot_of, live, place = route
    tp_width = layer_input_rows.shape[1]
    table, rank, _ = adapter_down_matrices.shape
    grid, order = Grid(), Order()
    chunks = Chunks(grid, order, weights, tp_width, tile)
    alone = capacity - held
    if own.shape[1] != alone:
        own = pack([(place, alone)], [columns])

    def cut(part, parts, rows):
        return {"rows": rows, "first": tp_width * sum(parts[:part]) // 8, "width": tp_width * parts[part] // 8}

    a, b = (cut(i, OWN_CUTS, own) for i in range(2))
    chunks.run([a])
    chunks.across(a)
    low = low[0] + low[1]
    got = lax.ppermute(low, "tp", [(i, i ^ 2) for i in range(8)])
    their_columns, their_place = theirs
    seats, from_columns = [(jnp.where(their_place >= 0, held - 1 - their_place, -1), held)], [their_columns]
    if held > alone:
        seats.append((place - alone, held - alone))
        from_columns.append(columns)
    seats[0] = (order.tie(seats[0][0]), held)
    shared = order.mark = pack(seats, from_columns)
    c, d, e = (cut(i, SHARED_CUTS, shared) for i in range(3))
    (got,) = chunks.run([c], done=[got])
    chunks.across(c)
    low = low + got
    got = lax.ppermute(low, "tp", [(i, i ^ 4) for i in range(8)])
    (got,) = chunks.run(to_keep=a, done=[got])
    low = low + got
    chunks.along(a)
    chunks.run([d])
    chunks.across(d)
    (a["parts"],) = chunks.run([b], c, [a["parts"]])
    chunks.across(b)
    chunks.along(c)
    chunks.run([e], flops=5 * HIDE)
    chunks.finish(a, False)
    chunks.across(e)
    (c["parts"],) = chunks.run(to_keep=d, done=[c["parts"]])
    chunks.along(d)
    chunks.run(to_keep=b)
    low = order.tie(low)
    reduced, back = low_rank_split(low, live)
    other, mine, contribution = rank_products(
        grid.core,
        spread(reduced, slot_of),
        spread(back, slot_of),
        spread(back, adapter_of),
        columns,
        layer_input_rows,
        adapter_down_matrices.reshape(table * rank, -1),
    )
    d["parts"], b["same"], b["other"], other, order.mark = lax.optimization_barrier(
        (d["parts"], b["same"], b["other"], other, contribution)
    )
    chunks.along(b)
    got = lax.ppermute(other, "dp", [(0, 1), (1, 0)])
    chunks.finish(c, True)
    b["parts"], c["moved"], got = chunks.run(to_keep=e, done=[b["parts"], c["moved"], got])
    chunks.along(e)
    chunks.finish(d, True)
    chunks.finish(b, False)
    owned = (order.tie(mine) + f32(got)).reshape(table // 2, rank, -1)
    owned_down, owned_up = owned[..., :tp_width], owned[..., tp_width:]
    order.mark = owned_down
    chunks.finish(e, True)

    kept = jnp.concatenate([a["sum"], b["sum"]], axis=1)
    if held > alone:
        rest = jnp.concatenate([k["sum"][: held - alone] for k in (c, d, e)], axis=1)
        kept = jnp.concatenate([kept, rest], axis=0)
    arrived = jnp.where(grid.u < 2, kept, jnp.concatenate([k["moved"] for k in (c, d, e)], axis=1))
    pick = seated(jnp.where(grid.u < 2, place, held - 1 - place), live, 0, held)
    base = dot(pick, arrived, ((0,), (0,)))
    input_gradient = jnp.where(live[:, None], base + ADAPTER_SCALE * contribution, 0.0).astype(jnp.bfloat16)
    return input_gradient, owned_down, owned_up


def rotation(groups, k, d):
    return [(2 * g + c, (g + k) % groups * 2 + (c + d) % 2) for g in range(groups) for c in range(2)]


def grid_body(
    layer_input_rows,
    cotangent,
    frozen_up_matrix,
    adapter_down_matrices,
    adapter_up_matrices,
    row_adapter_index,
    counts,
    offsets,
    gradient_owner_slot,
):
    count = layer_input_rows.shape[0]
    mine = jnp.sum(counts)
    here = jnp.stack([mine, mine]).reshape(2, 1)
    groups = lax.axis_size("dom")
    found = [lax.ppermute(here, ("dom", "dp"), rotation(groups, k, d)) for k in range(1, groups) for d in range(2)]
    args = (layer_input_rows, cotangent.T, frozen_up_matrix.T, adapter_down_matrices, adapter_up_matrices)
    sizes = [(count * c // 12, count * h // 12, tile) for c, h, tile in SIZES]
    row_adapter_index, _ = lax.optimization_barrier((row_adapter_index, here))
    route = routing(row_adapter_index, counts, offsets, gradient_owner_slot)
    theirs = tuple(lax.ppermute(v, "dp", [(0, 1), (1, 0)]) for v in (args[1], route[3]))
    low = low_rank_partial(layer_input_rows, args[1], adapter_down_matrices, adapter_up_matrices, route[0])
    low = low, lax.ppermute(low, "tp", [(i, i ^ 1) for i in range(8)])
    own = pack([(route[3], sizes[0][0] - sizes[0][1])], [args[1]])
    totals = [mine, jnp.max(theirs[1]) + 1] + [f[0, 0] for f in found]
    most = functools.reduce(jnp.maximum, totals)
    both = functools.reduce(jnp.maximum, [totals[2 * k] + totals[2 * k + 1] for k in range(groups)])
    branch = jnp.zeros((), jnp.int32)
    for capacity, held, _ in sizes[:-1]:
        branch = branch + ((both > capacity) | (most > held)).astype(jnp.int32)
    steps = [functools.partial(packed_step, *size) for size in sizes]
    if len(steps) == 1:
        return steps[0](args, route, theirs, low, own)
    return lax.switch(branch, steps, args, route, theirs, low, own)


def general_body(
    layer_input_rows,
    cotangent,
    frozen_up_matrix,
    adapter_down_matrices,
    adapter_up_matrices,
    row_adapter_index,
    counts,
    offsets,
    gradient_owner_slot,
):
    table, rank, _ = adapter_down_matrices.shape
    core = lax.axis_index("dp")
    adapter_of, slot_of, live, _ = routing(row_adapter_index, counts, offsets, gradient_owner_slot)
    partial = low_rank_partial(
        layer_input_rows, cotangent.T, adapter_down_matrices, adapter_up_matrices, adapter_of
    )
    reduced, back = low_rank_split(lax.psum(partial, "tp"), live)
    weights = lax.all_gather(frozen_up_matrix, "dp", axis=0, tiled=True)
    partial = dot(cotangent, weights, ((1,), (1,))).astype(jnp.bfloat16)
    base = lax.psum_scatter(partial, "tp", scatter_dimension=1, tiled=True).astype(jnp.float32)
    pairs = [(spread(reduced, slot_of), cotangent.T, 1), (spread(back, slot_of), layer_input_rows, 0)]
    owned_up, owned_down = split_gradients(*owned_gradients(core, pairs), pairs, rank)
    contribution = dot(
        spread(back, adapter_of), adapter_down_matrices.reshape(table * rank, -1), ((0,), (0,))
    )
    input_gradient = jnp.where(live[:, None], base + ADAPTER_SCALE * contribution, 0.0).astype(jnp.bfloat16)
    return input_gradient, owned_down, owned_up


def solution(mesh):
    in_specs = (
        P(("dom", "dp"), "tp"),
        P(("dom", "dp"), "tp"),
        P("dp", "tp"),
        P("dom", None, "tp"),
        P("dom", None, "tp"),
        P(("dom", "dp")),
        P(("dom", "dp"), None),
        P(("dom", "dp"), None),
        P("dom"),
    )
    out_specs = (P(("dom", "dp"), "tp"), P(("dom", "dp"), None, "tp"), P(("dom", "dp"), None, "tp"))
    body = grid_body if mesh.shape["tp"] == 8 and mesh.shape["dp"] == 2 else general_body
    return jax.shard_map(body, mesh=mesh, in_specs=in_specs, out_specs=out_specs, check_vma=False)
```

```python
import functools

import jax
import jax.numpy as jnp
from jax import lax
from jax.experimental import pallas as pl
from jax.experimental.pallas import tpu as pltpu
from jax.sharding import PartitionSpec as P

BLOCK = 128
ADAPTER_SCALE = 0.5
VMEM_LIMIT = 36 << 20
PACK_LIMIT = 56 << 20
VMEM_SPARE = 4 << 20
HIDE = 2 * 10**9
PIECE = 1280
SIZES = ((18, 11, 4096), (24, 12, 256))
OWN_CUTS = (5, 3)
SHARED_CUTS = (3, 3, 2)


def dot(a, b, dims):
    return lax.dot_general(a, b, (dims, ((), ())), preferred_element_type=jnp.float32)


def project(weights, starts, tasks, after=None, most=512, flops=0):
    picked = starts.shape[1]
    pieces, _, filled = tasks[0][0].shape
    length = weights.shape[0] // pieces
    row_operands = []
    for task in tasks:
        if not any(task[0] is r for r in row_operands):
            row_operands.append(task[0])
    addends = [t[4][0] for t in tasks if t[4] is not None]
    out_shape, scratch, nbytes = [], [], 0
    for rows, _, _, width, addend in tasks:
        count, wide = rows.shape[1], picked * width
        shapes = [(count, wide)] if addend is None else [(count, width)] * picked
        out_shape += [jax.ShapeDtypeStruct(shape, jnp.bfloat16) for shape in shapes]
        scratch += [
            pltpu.VMEM((pieces, filled, wide), jnp.bfloat16),
            pltpu.VMEM((count, wide), jnp.float32),
            pltpu.SemaphoreType.DMA((pieces, picked)),
        ]
        nbytes += pieces * filled * wide * 2 + count * wide * 4
        if addend is not None:
            scratch += [pltpu.VMEM((count, wide), jnp.bfloat16), pltpu.SemaphoreType.DMA((picked,))]
            nbytes += count * wide * 2

    def kernel(starts_ref, weights_ref, *refs):
        refs = list(refs)

        def take(n):
            return [refs.pop(0) for _ in range(n)]

        row_refs, addend_refs = take(len(row_operands)), take(len(addends))
        if after is not None:
            take(1)
        outs, jobs = take(len(out_shape)), []
        for rows, which, first, width, addend in tasks:
            rows_ref = row_refs[next(i for i, r in enumerate(row_operands) if r is rows)]
            out_refs = [outs.pop(0) for _ in range(1 if addend is None else picked)]
            weights_here, total, weight_sems = take(3)
            wide = picked * width

            def copies(p, which=which, first=first, width=width, weights_here=weights_here, weight_sems=weight_sems):
                depths = pl.ds(pl.multiple_of(p * length, 16), length)
                found = []
                for i in range(picked):
                    begin = pl.multiple_of(starts_ref[which, i] + first, 128)
                    source = weights_ref.at[depths, pl.ds(begin, width)]
                    target = weights_here.at[p, pl.ds(0, length), pl.ds(i * width, width)]
                    found.append(pltpu.make_async_copy(source, target, weight_sems.at[p, i]))
                return found

            for p in range(pieces):
                for copy in copies(p):
                    copy.start()
            addend_copies, addend_here = [], None
            if addend is not None:
                addend_here, addend_sems = take(2)
                addend_ref = addend_refs.pop(0)
                for i in range(picked):
                    source = addend_ref.at[:, pl.ds(i * (addend[0].shape[1] // picked) + addend[1], width)]
                    target = addend_here.at[:, pl.ds(i * width, width)]
                    addend_copies.append(pltpu.make_async_copy(source, target, addend_sems.at[i]))
                    addend_copies[i].start()
            jobs.append((rows_ref, weights_here, total, copies, addend_copies, addend_here, out_refs, wide))
        for rows_ref, weights_here, total, copies, addend_copies, addend_here, out_refs, wide in jobs:
            for p in range(pieces):
                weights_here[p, length:, :] = jnp.zeros((filled - length, wide), jnp.bfloat16)
            total[...] = jnp.zeros_like(total)

            tile = next(t for t in range(min(most, wide), 0, -128) if wide % t == 0)

            def step(p, carry, rows_ref=rows_ref, weights_here=weights_here, total=total, copies=copies, tile=tile, wide=wide):
                for copy in copies(p):
                    copy.wait()

                def columns(j, carry):
                    part = pl.ds(pl.multiple_of(j * tile, 128), tile)
                    total[:, part] += dot(rows_ref[p], weights_here[p, :, part], ((1,), (0,)))
                    return carry

                return lax.fori_loop(0, wide // tile, columns, carry)

            lax.fori_loop(0, pieces, step, 0)
            whole = total[...]
            for copy in addend_copies:
                copy.wait()
            if addend_copies:
                whole = whole + addend_here[...].astype(jnp.float32)
            for i, out_ref in enumerate(out_refs):
                out_ref[...] = whole[:, i * out_ref.shape[1] : (i + 1) * out_ref.shape[1]].astype(jnp.bfloat16)

    vmem, anywhere = pl.BlockSpec(memory_space=pltpu.VMEM), pl.BlockSpec(memory_space=pl.ANY)
    hbm = pl.BlockSpec(memory_space=pltpu.HBM)
    extra = addends + ([after] if after is not None else [])
    return pl.pallas_call(
        kernel,
        in_specs=[pl.BlockSpec(memory_space=pltpu.SMEM), hbm] + [vmem] * len(row_operands) + [anywhere] * len(extra),
        out_specs=[vmem] * len(out_shape),
        out_shape=out_shape,
        scratch_shapes=scratch,
        compiler_params=pltpu.CompilerParams(vmem_limit_bytes=max(nbytes + VMEM_SPARE, VMEM_LIMIT)),
        cost_estimate=pl.CostEstimate(flops=flops, bytes_accessed=1 << 14, transcendentals=0),
    )(starts, weights, *row_operands, *extra)


def pack(seats, columns):
    held, count = seats[0][1], seats[0][0].shape[0]
    depth = columns[0].shape[0]
    pieces = next(n for n in range(1, depth) if depth % (16 * n) == 0 and depth // n <= PIECE)
    length = depth // pieces
    filled = -(-length // 128) * 128
    heights = [height for _, height in seats]

    def kernel(*refs):
        seat_refs, refs = refs[: len(seats)], refs[len(seats) :]
        column_refs, (out_ref, *picks) = refs[: len(seats)], refs[len(seats) :]

        @pl.when(pl.program_id(0) == 0)
        def _():
            for seat_ref, pick_ref in zip(seat_refs, picks):
                number = lax.broadcasted_iota(jnp.int32, pick_ref.shape, 0)
                pick_ref[...] = jnp.where(number == seat_ref[...], 1.0, 0.0).astype(jnp.bfloat16)

        total = dot(picks[0][...], column_refs[0][...], ((1,), (1,)))
        out_ref[0, :, :length] = total.astype(jnp.bfloat16)
        for i in range(1, len(seats)):
            more = dot(picks[i][...], column_refs[i][...], ((1,), (1,)))
            out_ref[0, : heights[i], :length] = (total[: heights[i]] + more).astype(jnp.bfloat16)
        out_ref[0, :, length:] = jnp.zeros((held, filled - length), jnp.bfloat16)

    return pl.pallas_call(
        kernel,
        grid=(pieces,),
        in_specs=[pl.BlockSpec((1, count), lambda k: (0, 0)) for _ in seats]
        + [pl.BlockSpec((length, count), lambda k: (k, 0)) for _ in seats],
        out_specs=pl.BlockSpec((1, held, filled), lambda k: (k, 0, 0)),
        out_shape=jax.ShapeDtypeStruct((pieces, held, filled), jnp.bfloat16),
        scratch_shapes=[pltpu.VMEM((height, count), jnp.bfloat16) for height in heights],
        compiler_params=pltpu.CompilerParams(vmem_limit_bytes=PACK_LIMIT),
        cost_estimate=pl.CostEstimate(flops=1 << 20, bytes_accessed=1 << 14, transcendentals=0),
    )(*[seat[None, :] for seat, _ in seats], *columns)


class Grid:
    def __init__(self):
        self.core = lax.axis_index("dp")
        tp = lax.axis_index("tp")
        self.y = tp % 2
        self.u = jnp.where(self.core == 0, tp // 2, 3 - tp // 2)

    @staticmethod
    def at(core, u, y):
        return core * 8 + (u if core == 0 else 3 - u) * 2 + y

    def send(self, value, move):
        pairs = []
        for core in range(2):
            for u in range(4):
                for y in range(2):
                    to = move(core, u, y)
                    if to is not None:
                        pairs.append((self.at(core, u, y), self.at(*to)))
        return lax.ppermute(value, ("dp", "tp"), pairs)

    def across(self, value):
        return self.send(value, lambda c, u, y: (c, u, 1 - y))

    def along(self, value, ends, idle):
        return self.send(value, lambda c, u, y: (c, ends[u], y) if u in ends else idle(c, u, y))

    @staticmethod
    def none(c, u, y):
        return None

    @staticmethod
    def other_core(c, u, y):
        return 1 - c, 3 - u, y

    def to_other_core(self, value):
        return self.send(value, self.other_core)

    def blocks(self, y, tp_width):
        starts = []
        for k in range(2):
            u = (self.u + k) % 2
            starts.append((jnp.where(self.core == 0, u, 1 - u) * 2 + y) * tp_width)
        return jnp.stack(starts).astype(jnp.int32)


class Order:
    def __init__(self):
        self.mark = None

    def tie(self, value):
        if self.mark is None:
            return value
        return lax.optimization_barrier((value, self.mark))[0]


def f32(value):
    return value.astype(jnp.float32)


class Chunks:
    def __init__(self, grid, order, weights, tp_width, tile):
        self.grid, self.order, self.weights, self.tile = grid, order, weights, tile
        self.starts = jnp.stack([grid.blocks(1 - grid.y, tp_width), grid.blocks(grid.y, tp_width)])

    def run(self, to_send=(), to_keep=None, done=(), flops=0):
        tasks = [(k["rows"], 0, k["first"], k["width"], None) for k in to_send]
        if to_keep is not None:
            across, column = to_keep["across"]
            tasks.append((to_keep["rows"], 1, to_keep["first"], to_keep["width"], (self.order.tie(across), column)))
        flops = flops or (HIDE if to_keep is not None else 1 << 20)
        values = project(self.weights, self.order.tie(self.starts), tasks, self.order.mark, self.tile, flops)
        values, done = lax.optimization_barrier((values, tuple(done)))
        self.order.mark = values[-1]
        for chunk, value in zip(to_send, values):
            chunk["product"] = value
        if to_keep is not None:
            to_keep["same"], to_keep["other"] = values[-2:]
        return done

    def across(self, chunk):
        chunk["across"] = (self.grid.across(chunk["product"]), 0)

    def along(self, chunk):
        grid, same, other = self.grid, chunk["same"], chunk["other"]
        chunk["parts"] = (
            grid.along(same, {3: 1, 2: 0}, grid.other_core),
            grid.along(other, {3: 0, 2: 1}, grid.other_core),
            grid.along(other, {1: 0, 0: 1}, grid.none),
        )

    def finish(self, chunk, moved):
        total = f32(self.order.tie(chunk["same"]))
        for part in chunk["parts"]:
            total = total + f32(part)
        chunk["sum"] = self.order.mark = total.astype(jnp.bfloat16)
        if moved:
            chunk["moved"] = self.grid.to_other_core(chunk["sum"])


def low_rank_partial(layer_input_rows, columns, down, up, adapter_of):
    table, rank, _ = down.shape
    count = layer_input_rows.shape[0]
    down_all = dot(down.reshape(table * rank, -1), layer_input_rows, ((1,), (1,)))
    back_all = dot(up.reshape(table * rank, -1), columns, ((1,), (0,)))

    def pick(wide):
        return jnp.sum(jnp.where(adapter_of[:, None, :], wide.reshape(table, rank, count), 0.0), axis=0)

    return jnp.concatenate([pick(down_all), pick(back_all)], axis=0)


def low_rank_split(total, live):
    rank = total.shape[0] // 2
    total = jnp.where(live[None, :], total, 0.0).astype(jnp.bfloat16)
    return total[:rank], total[rank:]


def spread(low, chosen):
    rank, count = low.shape
    wide = jnp.where(chosen[:, None, :], low[None, :, :], jnp.zeros((), low.dtype))
    return wide.reshape(chosen.shape[0] * rank, count)


def owned_gradients(core, pairs):
    totals = [ADAPTER_SCALE * dot(wide, values, ((1,), (contract,))) for wide, values, contract in pairs]
    half = totals[0].shape[0] // 2

    def part(total, which):
        return lax.dynamic_slice_in_dim(total, which * half, half, 0)

    other = jnp.concatenate([part(t, 1 - core).astype(jnp.bfloat16) for t in totals], axis=1)
    got = lax.ppermute(other, "dp", [(0, 1), (1, 0)])
    mine = jnp.concatenate([part(t, core) for t in totals], axis=1)
    return mine, got


def split_gradients(mine, got, pairs, rank):
    total = mine + f32(got)
    half, first = total.shape[0], 0
    owned = []
    for _, values, contract in pairs:
        width = values.shape[1 - contract]
        owned.append(total[:, first : first + width].reshape(half // rank, rank, width))
        first += width
    return owned


def rank_products(core, reduced, back, back_by_adapter, columns, values, down):
    width, depth = values.shape[1], columns.shape[0]
    half = reduced.shape[0] // 2

    def kernel(core_ref, reduced_ref, back_ref, by_adapter_ref, columns_ref, values_ref, down_ref, *outs):
        other_ref, mine_ref, row_ref = outs
        for out_ref, which in ((other_ref, 1 - core_ref[0]), (mine_ref, core_ref[0])):
            part = pl.ds(pl.multiple_of(which * half, 16), half)
            out_ref[:, :width] = (ADAPTER_SCALE * dot(back_ref[part], values_ref[...], ((1,), (0,)))).astype(out_ref.dtype)
            out_ref[:, width:] = (ADAPTER_SCALE * dot(reduced_ref[part], columns_ref[...], ((1,), (1,)))).astype(
                out_ref.dtype
            )
        row_ref[...] = dot(by_adapter_ref[...], down_ref[...], ((0,), (0,)))

    vmem = pl.BlockSpec(memory_space=pltpu.VMEM)
    return pl.pallas_call(
        kernel,
        in_specs=[pl.BlockSpec(memory_space=pltpu.SMEM)] + [vmem] * 6,
        out_specs=[vmem] * 3,
        out_shape=[
            jax.ShapeDtypeStruct((half, width + depth), jnp.bfloat16),
            jax.ShapeDtypeStruct((half, width + depth), jnp.float32),
            jax.ShapeDtypeStruct(values.shape, jnp.float32),
        ],
        compiler_params=pltpu.CompilerParams(vmem_limit_bytes=VMEM_LIMIT),
        cost_estimate=pl.CostEstimate(flops=1 << 20, bytes_accessed=1 << 14, transcendentals=0),
    )(core.astype(jnp.int32)[None], reduced, back, back_by_adapter, columns, values, down)


def routing(row_adapter_index, counts, offsets, gradient_owner_slot):
    table = counts.shape[1]
    numbers = jnp.arange(table, dtype=jnp.int32)
    adapter_of = row_adapter_index[None, :] == numbers[:, None]
    ahead = jnp.sum(jnp.where(offsets[0][None, :] < offsets[0][:, None], counts[0][None, :], 0), axis=1)

    def of_row(values):
        return jnp.sum(jnp.where(adapter_of, values[:, None], 0), axis=0)

    slot_of = of_row(gradient_owner_slot)[None, :] == numbers[:, None]
    since = jnp.arange(row_adapter_index.shape[0], dtype=jnp.int32) - of_row(offsets[0] * BLOCK)
    live = (row_adapter_index < table) & (since >= 0) & (since < of_row(counts[0]))
    place = jnp.where(live, of_row(ahead) + since, -1)
    return adapter_of, slot_of, live, place


def seated(place, live, first, held):
    seats = first + jnp.arange(held, dtype=jnp.int32)
    return ((place[None, :] == seats[:, None]) & live[None, :]).astype(jnp.bfloat16)


def packed_step(capacity, held, tile, args, route, theirs, low, own):
    layer_input_rows, columns, weights, adapter_down_matrices, adapter_up_matrices = args
    adapter_of, slot_of, live, place = route
    tp_width = layer_input_rows.shape[1]
    table, rank, _ = adapter_down_matrices.shape
    grid, order = Grid(), Order()
    chunks = Chunks(grid, order, weights, tp_width, tile)
    alone = capacity - held
    if own.shape[1] != alone:
        own = pack([(place, alone)], [columns])

    def cut(part, parts, rows):
        return {"rows": rows, "first": tp_width * sum(parts[:part]) // 8, "width": tp_width * parts[part] // 8}

    a, b = (cut(i, OWN_CUTS, own) for i in range(2))
    chunks.run([a])
    chunks.across(a)
    low = low[0] + low[1]
    got = lax.ppermute(low, "tp", [(i, i ^ 2) for i in range(8)])
    their_columns, their_place = theirs
    seats, from_columns = [(jnp.where(their_place >= 0, held - 1 - their_place, -1), held)], [their_columns]
    if held > alone:
        seats.append((place - alone, held - alone))
        from_columns.append(columns)
    seats[0] = (order.tie(seats[0][0]), held)
    shared = order.mark = pack(seats, from_columns)
    c, d, e = (cut(i, SHARED_CUTS, shared) for i in range(3))
    (got,) = chunks.run([c], done=[got])
    chunks.across(c)
    low = low + got
    got = lax.ppermute(low, "tp", [(i, i ^ 4) for i in range(8)])
    (got,) = chunks.run(to_keep=a, done=[got])
    low = low + got
    chunks.along(a)
    chunks.run([d])
    chunks.across(d)
    (a["parts"],) = chunks.run([b], c, [a["parts"]])
    chunks.across(b)
    chunks.along(c)
    chunks.run([e], flops=5 * HIDE)
    chunks.finish(a, False)
    chunks.across(e)
    (c["parts"],) = chunks.run(to_keep=d, done=[c["parts"]])
    chunks.along(d)
    chunks.run(to_keep=b)
    low = order.tie(low)
    reduced, back = low_rank_split(low, live)
    other, mine, contribution = rank_products(
        grid.core,
        spread(reduced, slot_of),
        spread(back, slot_of),
        spread(back, adapter_of),
        columns,
        layer_input_rows,
        adapter_down_matrices.reshape(table * rank, -1),
    )
    d["parts"], b["same"], b["other"], other, order.mark = lax.optimization_barrier(
        (d["parts"], b["same"], b["other"], other, contribution)
    )
    chunks.along(b)
    got = lax.ppermute(other, "dp", [(0, 1), (1, 0)])
    chunks.finish(c, True)
    b["parts"], c["moved"], got = chunks.run(to_keep=e, done=[b["parts"], c["moved"], got])
    chunks.along(e)
    chunks.finish(d, True)
    chunks.finish(b, False)
    owned = (order.tie(mine) + f32(got)).reshape(table // 2, rank, -1)
    owned_down, owned_up = owned[..., :tp_width], owned[..., tp_width:]
    order.mark = owned_down
    chunks.finish(e, True)

    kept = jnp.concatenate([a["sum"], b["sum"]], axis=1)
    if held > alone:
        rest = jnp.concatenate([k["sum"][: held - alone] for k in (c, d, e)], axis=1)
        kept = jnp.concatenate([kept, rest], axis=0)
    arrived = jnp.where(grid.u < 2, kept, jnp.concatenate([k["moved"] for k in (c, d, e)], axis=1))
    pick = seated(jnp.where(grid.u < 2, place, held - 1 - place), live, 0, held)
    base = dot(pick, arrived, ((0,), (0,)))
    input_gradient = jnp.where(live[:, None], base + ADAPTER_SCALE * contribution, 0.0).astype(jnp.bfloat16)
    return input_gradient, owned_down, owned_up


def rotation(groups, k, d):
    return [(2 * g + c, (g + k) % groups * 2 + (c + d) % 2) for g in range(groups) for c in range(2)]


def grid_body(
    layer_input_rows,
    cotangent,
    frozen_up_matrix,
    adapter_down_matrices,
    adapter_up_matrices,
    row_adapter_index,
    counts,
    offsets,
    gradient_owner_slot,
):
    count = layer_input_rows.shape[0]
    mine = jnp.sum(counts)
    here = jnp.stack([mine, mine]).reshape(2, 1)
    groups = lax.axis_size("dom")
    found = [lax.ppermute(here, ("dom", "dp"), rotation(groups, k, d)) for k in range(1, groups) for d in range(2)]
    args = (layer_input_rows, cotangent.T, frozen_up_matrix.T, adapter_down_matrices, adapter_up_matrices)
    sizes = [(count * c // 12, count * h // 12, tile) for c, h, tile in SIZES]
    row_adapter_index, _ = lax.optimization_barrier((row_adapter_index, here))
    route = routing(row_adapter_index, counts, offsets, gradient_owner_slot)
    theirs = tuple(lax.ppermute(v, "dp", [(0, 1), (1, 0)]) for v in (args[1], route[3]))
    low = low_rank_partial(layer_input_rows, args[1], adapter_down_matrices, adapter_up_matrices, route[0])
    low = low, lax.ppermute(low, "tp", [(i, i ^ 1) for i in range(8)])
    own = pack([(route[3], sizes[0][0] - sizes[0][1])], [args[1]])
    totals = [mine, jnp.max(theirs[1]) + 1] + [f[0, 0] for f in found]
    most = functools.reduce(jnp.maximum, totals)
    both = functools.reduce(jnp.maximum, [totals[2 * k] + totals[2 * k + 1] for k in range(groups)])
    branch = jnp.zeros((), jnp.int32)
    for capacity, held, _ in sizes[:-1]:
        branch = branch + ((both > capacity) | (most > held)).astype(jnp.int32)
    steps = [functools.partial(packed_step, *size) for size in sizes]
    if len(steps) == 1:
        return steps[0](args, route, theirs, low, own)
    return lax.switch(branch, steps, args, route, theirs, low, own)


def general_body(
    layer_input_rows,
    cotangent,
    frozen_up_matrix,
    adapter_down_matrices,
    adapter_up_matrices,
    row_adapter_index,
    counts,
    offsets,
    gradient_owner_slot,
):
    table, rank, _ = adapter_down_matrices.shape
    core = lax.axis_index("dp")
    adapter_of, slot_of, live, _ = routing(row_adapter_index, counts, offsets, gradient_owner_slot)
    partial = low_rank_partial(
        layer_input_rows, cotangent.T, adapter_down_matrices, adapter_up_matrices, adapter_of
    )
    reduced, back = low_rank_split(lax.psum(partial, "tp"), live)
    weights = lax.all_gather(frozen_up_matrix, "dp", axis=0, tiled=True)
    partial = dot(cotangent, weights, ((1,), (1,))).astype(jnp.bfloat16)
    base = lax.psum_scatter(partial, "tp", scatter_dimension=1, tiled=True).astype(jnp.float32)
    pairs = [(spread(reduced, slot_of), cotangent.T, 1), (spread(back, slot_of), layer_input_rows, 0)]
    owned_up, owned_down = split_gradients(*owned_gradients(core, pairs), pairs, rank)
    contribution = dot(
        spread(back, adapter_of), adapter_down_matrices.reshape(table * rank, -1), ((0,), (0,))
    )
    input_gradient = jnp.where(live[:, None], base + ADAPTER_SCALE * contribution, 0.0).astype(jnp.bfloat16)
    return input_gradient, owned_down, owned_up


def solution(mesh):
    in_specs = (
        P(("dom", "dp"), "tp"),
        P(("dom", "dp"), "tp"),
        P("dp", "tp"),
        P("dom", None, "tp"),
        P("dom", None, "tp"),
        P(("dom", "dp")),
        P(("dom", "dp"), None),
        P(("dom", "dp"), None),
        P("dom"),
    )
    out_specs = (P(("dom", "dp"), "tp"), P(("dom", "dp"), None, "tp"), P(("dom", "dp"), None, "tp"))
    body = grid_body if mesh.shape["tp"] == 8 and mesh.shape["dp"] == 2 else general_body
    return jax.shard_map(body, mesh=mesh, in_specs=in_specs, out_specs=out_specs, check_vma=False)
```
